256 devices in a mesh: nodes: 32 (over x, y, core), heads: 8 (over z).
Axes of the slice: x: 4, y: 4, z: 8, core: 2. Of those that a mesh axis runs over, the one named last changes fastest.
Arguments:
- node_states: bfloat16 [131072, 512], P('nodes'), may hold values from -6 to 6
- virtual_states: bfloat16 [32, 512], P('nodes'), may hold values from -6 to 6
- project_weight: bfloat16 [512, 1536], P(None, 'heads'), may hold values from -0.4375 to 0.4375
- output_weight: bfloat16 [512, 512], replicated, may hold values from -0.25 to 0.25
- expand_weight: bfloat16 [512, 2048], P(None, 'heads'), may hold values from -0.25 to 0.25
- expand_bias: float32 [2048], replicated, may hold values from -5 to 5
- contract_weight: bfloat16 [2048, 512], P('heads'), may hold values from -0.125 to 0.125
- neigh_source: int32 [1024, 4], P('nodes'), may hold values from 0 to 1023, as said below
- neigh_rows: int32 [1024, 4, 128], P('nodes'), may hold values from 0 to 127
- neigh_count: int32 [1024, 4], P('nodes'), may hold values from 1 to 128
- expander_source: int32 [1024, 4], P('nodes'), may hold values from 0 to 1023, as said below
- expander_rows: int32 [1024, 4, 128], P('nodes'), may hold values from 0 to 127, each once within a row
- expander_count: int32 [1024, 4], P('nodes'), may hold values from 112 to 128
Outputs:
- updated: bfloat16 [131072, 512], P(('nodes', 'heads'))
The draws below stay inside these ranges and needn't reach their ends.
Inputs may be any that keep to these rules, and one draw needn't show every extreme that they name: `neigh_source`: the neighbour tiles of block b have source block b - 1, b or b + 1 modulo 1024. `expander_source`: for the blocks of one index of nodes and any one index of nodes, at most 8 expander tiles have their source block there, naming at most 4 distinct source blocks; both bounds are reached.
All inputs are finite; a program needn't handle non-finite values.
Results may differ from the reference program's by a relative error of at most 0.012.
Values may be sent and summed in bfloat16 or wider, within the bound.
No kernel may reach another device: no remote copies, remote signals or barrier semaphores. Data moves between devices by JAX's collectives and lax.ppermute only.
A program may use at most 128 MiB of HBM per device.

```python
import jax
import jax.numpy as jnp
from jax import lax

D = 512
HEADS = 8
HEAD_DIM = 64
FF = 2048
BR = 128
NB_DEV = 32
VIRT = 32
NEIGH = 4
EXP_DEG = 4
BLOCKS = 1024
NODES = 131072
CAP = 8
BCAP = 4


def draw_neigh_source(key, part):
    key = jax.random.fold_in(key, 5)
    shift_by = jax.random.randint(key, (BLOCKS, NEIGH), -1, 2)
    block_ids = jnp.arange(BLOCKS, dtype=jnp.int32)[:, None]
    return jnp.mod(block_ids + shift_by, BLOCKS).astype(jnp.int32)


def draw_expander_source(key, part):
    key = jax.random.fold_in(key, 11)
    node_span = BLOCKS // NB_DEV
    tile_count = NB_DEV * EXP_DEG
    key_hot, key_turn, key_rank, key_blocks, key_rest = jax.random.split(key, 5)
    hot_node = jax.random.randint(key_hot, (node_span,), 0, node_span)
    rotation = jax.random.randint(key_turn, (node_span,), 0, node_span - 1)
    tile_rank = jax.vmap(lambda item: jax.random.permutation(item, tile_count))(jax.random.split(key_rank, node_span))
    hot_blocks = jax.vmap(lambda item: jax.random.permutation(item, NB_DEV))(jax.random.split(key_blocks, node_span))[:, :BCAP]
    rest_blocks = jax.random.randint(key_rest, (node_span, tile_count), 0, NB_DEV)
    is_hot = tile_rank < CAP
    other_place = jnp.mod(tile_rank - CAP + rotation[:, None], node_span - 1)
    other_node = other_place + (other_place >= hot_node[:, None]).astype(jnp.int32)
    owner_node = jnp.where(is_hot, hot_node[:, None], other_node)
    hot_pick = jnp.take_along_axis(hot_blocks, jnp.clip(tile_rank // 2, 0, BCAP - 1), axis=1)
    chosen = jnp.where(is_hot, hot_pick, rest_blocks)
    return (owner_node * NB_DEV + chosen).reshape(BLOCKS, EXP_DEG).astype(jnp.int32)


def set_ends(values, key, low, largest):
    extent = values.shape
    spot = [jax.random.randint(jax.random.fold_in(key, axis), (), 0, extent[axis]) for axis in range(len(extent))]
    values = values.at[tuple(spot)].set(low)
    longest = extent.index(max(extent))
    spot[longest] = (spot[longest] + 1) % extent[longest]
    return values.at[tuple(spot)].set(largest)


def block_scale(stream_key, dims, shards, low, largest):
    def one(dim, parts):
        steps = jax.random.uniform(jax.random.fold_in(jax.random.fold_in(stream_key, 6), dim), (parts,), jnp.float32, low / len(shards), largest / len(shards))
        return jnp.repeat(jnp.exp(steps), dims[dim] // parts).reshape((-1,) + (1,) * (len(dims) - dim - 1))

    loudness = one(*shards[0])
    for cut in shards[1:]:
        loudness = loudness * one(*cut)
    return loudness


def gaussian(rng, dims, width, most, pieces=(), kind=jnp.bfloat16):
    values = jax.random.normal(rng, dims, jnp.float32) * width
    if len(pieces) > 0:
        values = block_scale(rng, dims, pieces, -0.22, 0.18) * values
    return jnp.clip(values, min=-most, max=most).astype(kind)


def setup_inputs(seed: int = 0) -> dict:
    keys = jax.random.split(jax.random.key(seed), 14)
    node_states = gaussian(keys[0], (NODES, D), 1.0, 6.0, ((0, 32),))
    virtual_states = gaussian(keys[1], (VIRT, D), 1.0, 6.0, ((0, 32),))
    project_weight = gaussian(keys[2], (D, 3 * HEADS * HEAD_DIM), (D // 3) ** -0.5, 0.4375, ((1, 8),))
    output_weight = gaussian(keys[3], (D, D), D ** -0.5, 0.25)
    expand_weight = gaussian(keys[4], (D, FF), D ** -0.5, 0.25, ((1, 8),))
    expand_bias = gaussian(keys[5], (FF,), 1.0, 5.0, (), jnp.float32)
    contract_weight = gaussian(keys[6], (FF, D), FF ** -0.5, 0.125, ((0, 8),))
    neigh_source = draw_neigh_source(jax.random.fold_in(keys[13], 71), 0)
    neigh_rows = set_ends(jax.random.randint(keys[8], (BLOCKS, NEIGH, BR), 0, BR), jax.random.fold_in(keys[8], 1), 0, BR - 1).astype(jnp.int32)
    neigh_count = set_ends(jax.random.randint(keys[9], (BLOCKS, NEIGH), 1, BR + 1), jax.random.fold_in(keys[9], 1), 1, BR).astype(jnp.int32)
    expander_source = draw_expander_source(jax.random.fold_in(keys[13], 71), 0)
    expander_rows = jax.vmap(lambda own: jax.random.permutation(own, BR))(jax.random.split(keys[11], BLOCKS * EXP_DEG)).reshape((BLOCKS, EXP_DEG, BR)).astype(jnp.int32)
    expander_count = set_ends(jax.random.randint(keys[12], (BLOCKS, EXP_DEG), BR - BR // 8, BR + 1), jax.random.fold_in(keys[12], 1), BR - BR // 8, BR).astype(jnp.int32)
    return {"node_states": node_states, "virtual_states": virtual_states, "project_weight": project_weight, "output_weight": output_weight, "expand_weight": expand_weight, "expand_bias": expand_bias, "contract_weight": contract_weight, "neigh_source": neigh_source, "neigh_rows": neigh_rows, "neigh_count": neigh_count, "expander_source": expander_source, "expander_rows": expander_rows, "expander_count": expander_count}


eps_norm = 1e-05
clip_level = 5.0

def layer_norm(values):
    values = values.astype(jnp.float32)
    center = values - lax.optimization_barrier(jnp.mean(values, axis=-1, keepdims=True))
    spread = lax.optimization_barrier(jnp.mean(center * center, axis=-1, keepdims=True))
    return center * lax.rsqrt(spread + eps_norm)

def attend_exact(query, graph_pairs, usable, virtual_pairs):
    scaling = HEAD_DIM ** (-0.5)
    query = query.astype(jnp.float32)
    graph_pairs = graph_pairs.astype(jnp.float32)
    virtual_pairs = virtual_pairs.astype(jnp.float32)
    graph_score = jnp.einsum('nbhd,ngbhd->ngbh', query, graph_pairs[..., 0, :]) * scaling
    virtual_score = jnp.einsum('nbhd,vhd->nbvh', query, virtual_pairs[:, :, 0, :]) * scaling
    graph_weight = jnp.where(usable[..., None], jnp.exp(jnp.clip(graph_score, -clip_level, clip_level)), 0.0)
    virtual_weight = jnp.exp(jnp.clip(virtual_score, -clip_level, clip_level))
    summed = lax.optimization_barrier(jnp.sum(graph_weight, axis=1)) + lax.optimization_barrier(jnp.sum(virtual_weight, axis=2))
    graph_prob = (graph_weight / summed[:, None]).astype(jnp.bfloat16).astype(jnp.float32)
    virtual_prob = (virtual_weight / summed[:, :, None]).astype(jnp.bfloat16).astype(jnp.float32)
    result = jnp.einsum('ngbh,ngbhd->nbhd', graph_prob, graph_pairs[..., 1, :])
    result = result + jnp.einsum('nbvh,vhd->nbhd', virtual_prob, virtual_pairs[:, :, 1, :])
    return result.astype(jnp.bfloat16)

def reference(node_states, virtual_states, project_weight, output_weight, expand_weight, expand_bias, contract_weight, neigh_source, neigh_rows, neigh_count, expander_source, expander_rows, expander_count):
    normed = layer_norm(node_states).astype(jnp.bfloat16)
    projected = jnp.dot(normed, project_weight, preferred_element_type=jnp.float32).astype(jnp.bfloat16)
    projected = projected.reshape(NODES, HEADS, 3, HEAD_DIM)
    query = projected[:, :, 0, :]
    keyval = projected[:, :, 1:, :]
    virtual_normed = layer_norm(virtual_states).astype(jnp.bfloat16)
    virtual_projected = jnp.dot(virtual_normed, project_weight, preferred_element_type=jnp.float32).astype(jnp.bfloat16)
    virtual_pairs = virtual_projected.reshape(VIRT, HEADS, 3, HEAD_DIM)[:, :, 1:, :]
    sources = jnp.concatenate([neigh_source, expander_source], axis=1)
    row_ids = jnp.concatenate([neigh_rows, expander_rows], axis=1)
    counts = jnp.concatenate([neigh_count, expander_count], axis=1)
    graph_keys = NEIGH + EXP_DEG

    def one_block(inputs):
        block_index, block_sources, block_rows, block_counts = inputs
        block_query = lax.dynamic_slice_in_dim(query, (block_index * BR).astype(jnp.int32), BR, 0)[None]
        graph_index = (block_sources[:, None] * BR + block_rows).astype(jnp.int32)
        pairs = jnp.take(keyval, graph_index.reshape(-1), axis=0).reshape(1, graph_keys, BR, HEADS, 2, HEAD_DIM)
        usable = (jnp.arange(BR, dtype=jnp.int32)[None, :] < block_counts[:, None])[None]
        return attend_exact(block_query, pairs, usable, virtual_pairs)[0]
    attended = lax.map(one_block, (jnp.arange(BLOCKS, dtype=jnp.int32), sources, row_ids, counts))
    attended = attended.reshape(NODES, D)
    residual = node_states.astype(jnp.float32) + jnp.dot(attended, output_weight, preferred_element_type=jnp.float32)
    normed_two = layer_norm(residual).astype(jnp.bfloat16)
    hidden = jax.nn.gelu(jnp.dot(normed_two, expand_weight, preferred_element_type=jnp.float32) + expand_bias, approximate=False).astype(jnp.bfloat16)
    updated = residual + jnp.dot(hidden, contract_weight, preferred_element_type=jnp.float32)
    return updated.astype(jnp.bfloat16)
```

```python
import functools

import jax
import jax.numpy as jnp
from jax import lax
from jax.experimental import pallas as pl
from jax.experimental.pallas import tpu as pltpu
from jax.sharding import PartitionSpec as P

HEAD_DIM = 64
BCAP = 4

eps_norm = 1e-05
clip_level = 5.0

f32 = jnp.float32
bf16 = jnp.bfloat16
VMEM_LIMIT = 56 * 2**20


def layer_norm(values):
    values = values.astype(f32)
    center = values - jnp.mean(values, axis=-1, keepdims=True)
    spread = jnp.mean(center * center, axis=-1, keepdims=True)
    return center * lax.rsqrt(spread + eps_norm)


def params():
    return pltpu.CompilerParams(vmem_limit_bytes=VMEM_LIMIT)


def project_kernel(x_ref, w_ref, query_ref, pack_ref, side_ref):
    head = HEAD_DIM

    @pl.when(pl.program_id(0) == 0)
    def _():
        weight = w_ref[...]
        side = jnp.concatenate([weight[:, :head], weight[:, 2 * head :]], axis=1)
        side_ref[...] = side.T

    normed = layer_norm(x_ref[...]).astype(bf16)
    sides = lax.dot_general(
        side_ref[...], normed, (((1,), (1,)), ((), ())), preferred_element_type=f32
    ).astype(bf16)
    keys = jnp.dot(normed, w_ref[:, head : 2 * head], preferred_element_type=f32).astype(bf16)
    query_ref[...] = sides[:head] * jnp.asarray(head**-0.5, bf16)
    rows = 2 * head
    for item in range(x_ref.shape[0] // rows):
        low = keys[item * rows : item * rows + head]
        high = keys[item * rows + head : (item + 1) * rows]
        pack_ref[item, :head, :] = jnp.concatenate([low, high], axis=1)
        pack_ref[item, head:, :] = sides[head:, item * rows : (item + 1) * rows]


def project(states, weight, step_rows):
    rows, features = states.shape
    wide = 2 * HEAD_DIM
    return pl.pallas_call(
        project_kernel,
        grid=(rows // step_rows,),
        in_specs=[
            pl.BlockSpec((step_rows, features), lambda i: (i, 0)),
            pl.BlockSpec(weight.shape, lambda i: (0, 0)),
        ],
        out_specs=[
            pl.BlockSpec((HEAD_DIM, step_rows), lambda i: (0, i)),
            pl.BlockSpec((step_rows // wide, wide, wide), lambda i: (i, 0, 0)),
        ],
        out_shape=[
            jax.ShapeDtypeStruct((HEAD_DIM, rows), bf16),
            jax.ShapeDtypeStruct((rows // wide, wide, wide), bf16),
        ],
        scratch_shapes=[pltpu.VMEM((wide, features), bf16)],
        compiler_params=params(),
        name="project",
    )(states, weight)


def select_kernel(wanted_ref, pack_ref, out_ref):
    count = out_ref.shape[0]
    base = pl.program_id(0) * count
    for item in range(count):
        out_ref[item] = pack_ref[wanted_ref[base + item]]


def select_blocks(wanted, packed, step_items):
    total = wanted.shape[0]
    return pl.pallas_call(
        select_kernel,
        grid_spec=pltpu.PrefetchScalarGridSpec(
            num_scalar_prefetch=1,
            grid=(total // step_items,),
            in_specs=[pl.BlockSpec(packed.shape, lambda i, s: (0, 0, 0))],
            out_specs=pl.BlockSpec((step_items,) + packed.shape[1:], lambda i, s: (i, 0, 0)),
        ),
        out_shape=jax.ShapeDtypeStruct((total,) + packed.shape[1:], bf16),
        compiler_params=params(),
        name="select_blocks",
    )(wanted, packed)


def wide_query(query):
    zero = jnp.zeros_like(query)
    return jnp.concatenate(
        [jnp.concatenate([query, zero], axis=1), jnp.concatenate([zero, query], axis=1)], axis=0
    )


def tile_terms(queries, blocks, rows, counts):
    head = HEAD_DIM
    lane = lax.broadcasted_iota(jnp.int32, (1, 2 * head), 1)
    spot = lax.broadcasted_iota(jnp.int32, (head, 2 * head), 0)
    tables = []
    total = None
    for tile, block in enumerate(blocks):
        scores = jnp.dot(block[:head], queries, preferred_element_type=f32)
        row = rows[tile : tile + 1]
        low = row < head
        chosen = jnp.where(low, scores[:, : 2 * head], scores[:, 2 * head :])
        hit = spot == jnp.where(low, row, row - head)
        score = jnp.sum(jnp.where(hit, chosen, 0.0), axis=0, keepdims=True)
        weight = jnp.exp(jnp.clip(score, -clip_level, clip_level))
        weight = jnp.where(lane < counts[tile], weight, 0.0)
        total = weight if total is None else total + weight
        tables.append(jnp.where(hit, jnp.where(low, weight, 0.0), 0.0).astype(bf16))
        tables.append(jnp.where(hit, jnp.where(low, 0.0, weight), 0.0).astype(bf16))
    values = jnp.concatenate([block[head:] for block in blocks], axis=1)
    summed = jnp.dot(values, jnp.concatenate(tables, axis=0), preferred_element_type=f32)
    return summed, total


def near_kernel(
    group, shift_ref, count_ref, query_ref, pack_ref, left_ref, right_ref, virtual_ref, rows_ref,
    sum_ref, total_ref, window_ref,
):
    head = HEAD_DIM
    blocks, tiles, wide = rows_ref.shape
    virtual_total = 32
    window_ref[0] = left_ref[...]
    window_ref[blocks + 1] = right_ref[...]

    def fill(block, _):
        window_ref[block + 1] = pack_ref[block]
        return 0

    lax.fori_loop(0, blocks, fill, 0, unroll=8)
    virtual_keys = virtual_ref[:virtual_total, :head]
    virtual_values = virtual_ref[head:, :virtual_total]

    def step(turn, _):
        for item in range(group):
            block = turn * group + item
            lanes = pl.ds(pl.multiple_of(block * wide, wide), wide)
            query = query_ref[:, lanes]
            tile_blocks = [window_ref[shift_ref[block * tiles + t]] for t in range(tiles)]
            counts = [count_ref[block * tiles + t] for t in range(tiles)]
            summed, total = tile_terms(wide_query(query), tile_blocks, rows_ref[block], counts)
            scores = jnp.dot(virtual_keys, query, preferred_element_type=f32)
            weights = jnp.exp(jnp.clip(scores, -clip_level, clip_level))
            total = total + jnp.sum(weights, axis=0, keepdims=True)
            summed = summed + jnp.dot(
                virtual_values, weights.astype(bf16), preferred_element_type=f32
            )
            sum_ref[:, lanes] = summed
            total_ref[:, lanes] = total
        return 0

    lax.fori_loop(0, blocks // group, step, 0)


def near_terms(shifts, counts, query, packed, left, right, virtual, rows, group):
    head, total = query.shape
    blocks = packed.shape[0]
    vmem = pl.BlockSpec(memory_space=pltpu.VMEM)
    smem = pl.BlockSpec(memory_space=pltpu.SMEM)
    return pl.pallas_call(
        functools.partial(near_kernel, group),
        in_specs=[smem, smem] + [vmem] * 6,
        out_specs=[vmem, vmem],
        out_shape=[
            jax.ShapeDtypeStruct((head, total), f32),
            jax.ShapeDtypeStruct((1, total), f32),
        ],
        scratch_shapes=[pltpu.VMEM((blocks + 2,) + packed.shape[1:], bf16)],
        compiler_params=params(),
        cost_estimate=pl.CostEstimate(
            flops=8 * 2**30, bytes_accessed=4 * 2**20, transcendentals=2**20
        ),
        name="near_terms",
    )(shifts, counts, query, packed, left, right, virtual, rows)


def far_kernel(
    group, slot_ref, count_ref, query_ref, reply_ref, rows_ref, sum_ref, total_ref, out_ref
):
    blocks, tiles, wide = rows_ref.shape
    share_blocks = blocks // out_ref.shape[0]

    def step(turn, _):
        for item in range(group):
            block = turn * group + item
            lanes = pl.ds(pl.multiple_of(block * wide, wide), wide)
            tile_blocks = [reply_ref[slot_ref[block * tiles + t]] for t in range(tiles)]
            counts = [count_ref[block * tiles + t] for t in range(tiles)]
            summed, total = tile_terms(
                wide_query(query_ref[:, lanes]), tile_blocks, rows_ref[block], counts
            )
            total = total + total_ref[:, lanes]
            result = (summed + sum_ref[:, lanes]) * (1.0 / total)
            inner = pl.ds(pl.multiple_of(lax.rem(block, share_blocks) * wide, wide), wide)
            out_ref[lax.div(block, share_blocks), :, inner] = result.astype(bf16)
        return 0

    lax.fori_loop(0, blocks // group, step, 0)


def far_terms(slots, counts, query, replies, rows, near_sum, near_total, shares, group):
    head, total = query.shape
    vmem = pl.BlockSpec(memory_space=pltpu.VMEM)
    smem = pl.BlockSpec(memory_space=pltpu.SMEM)
    return pl.pallas_call(
        functools.partial(far_kernel, group),
        in_specs=[smem, smem] + [vmem] * 5,
        out_specs=vmem,
        out_shape=jax.ShapeDtypeStruct((shares, head, total // shares), bf16),
        compiler_params=params(),
        name="far_terms",
    )(slots, counts, query, replies, rows, near_sum, near_total)


def tail_kernel(
    place_ref, att_ref, own_ref, output_ref, expand_ref, bias_ref, contract_ref, out_ref,
    normed_ref, sum_ref,
):
    step = pl.program_id(0)

    @pl.when(step == 0)
    def _():
        heads, head, rows = att_ref.shape
        attended = att_ref[...].reshape(heads * head, rows).T
        residual = own_ref[...].astype(f32) + jnp.dot(
            attended, output_ref[...], preferred_element_type=f32
        )
        normed_ref[...] = layer_norm(residual).astype(bf16)
        sum_ref[...] = residual

    inner = jnp.dot(normed_ref[...], expand_ref[...], preferred_element_type=f32) + bias_ref[...]
    hidden = (inner * 0.5) * (1.0 + lax.erf(inner * (0.5**0.5)))
    sum_ref[...] += jnp.dot(hidden.astype(bf16), contract_ref[...], preferred_element_type=f32)

    @pl.when(step == pl.num_programs(0) - 1)
    def _():
        out_ref[...] = sum_ref[...].astype(bf16)


def tail(place, regrouped, node_states, output_weight, expand, bias, contract):
    heads, head, rows = regrouped.shape
    features = heads * head
    parts, _, width = expand.shape
    return pl.pallas_call(
        tail_kernel,
        grid_spec=pltpu.PrefetchScalarGridSpec(
            num_scalar_prefetch=1,
            grid=(parts,),
            in_specs=[
                pl.BlockSpec(regrouped.shape, lambda i, s: (0, 0, 0)),
                pl.BlockSpec((rows, features), lambda i, s: (s[0], 0)),
                pl.BlockSpec(output_weight.shape, lambda i, s: (0, 0)),
                pl.BlockSpec((None, features, width), lambda i, s: (i, 0, 0)),
                pl.BlockSpec((None, 1, width), lambda i, s: (i, 0, 0)),
                pl.BlockSpec((None, width, features), lambda i, s: (i, 0, 0)),
            ],
            out_specs=pl.BlockSpec((rows, features), lambda i, s: (0, 0)),
            scratch_shapes=[pltpu.VMEM((rows, features), bf16), pltpu.VMEM((rows, features), f32)],
        ),
        out_shape=jax.ShapeDtypeStruct((rows, features), bf16),
        compiler_params=params(),
        name="tail",
    )(place, regrouped, node_states, output_weight, expand, bias, contract)


def ranked_blocks(present):
    size = present.shape[1]
    before = jnp.arange(size)[:, None] < jnp.arange(size)[None, :]
    return jnp.sum(jnp.where(present[:, :, None] & before[None], 1, 0), axis=1)


def local(
    node_states,
    virtual_states,
    project_weight,
    output_weight,
    expand_weight,
    expand_bias,
    contract_weight,
    neigh_source,
    neigh_rows,
    neigh_count,
    expander_source,
    expander_rows,
    expander_count,
):
    span = lax.axis_size("nodes")
    me = lax.axis_index("nodes")
    shares = lax.axis_size("heads")
    share = lax.axis_index("heads")
    blocks, neigh_tiles, block_rows = neigh_rows.shape
    features = node_states.shape[1]
    tile_count = expander_source.size
    all_blocks = blocks * span
    lanes = 128

    source = expander_source.reshape(1, tile_count)
    owner, place = source // blocks, source % blocks
    message = jnp.concatenate(
        [
            owner.astype(bf16),
            place.astype(bf16),
            virtual_states.reshape(features // lanes, lanes),
            jnp.zeros((2, lanes), bf16),
        ],
        axis=0,
    )
    message = jnp.broadcast_to(message[None], (span,) + message.shape)
    heard = lax.all_to_all(message, "nodes", split_axis=0, concat_axis=0, tiled=True)
    rightward = [(i, (i + 1) % span) for i in range(span)]
    leftward = [((i + 1) % span, i) for i in range(span)]
    left = lax.ppermute(node_states[-block_rows:], "nodes", rightward)
    right = lax.ppermute(node_states[:block_rows], "nodes", leftward)

    expand = lax.all_gather(expand_weight, "heads", axis=0)
    contract = lax.all_gather(contract_weight, "heads", axis=0)

    query, packed = project(node_states, project_weight, 512)

    local_ids = jnp.arange(blocks, dtype=jnp.int32)
    asked = jnp.where(heard[:, 0] == me.astype(bf16), heard[:, 1], jnp.asarray(-1, bf16))
    asked = asked.astype(jnp.int32)
    present = jnp.any(asked[:, :, None] == local_ids, axis=1)
    rank = ranked_blocks(present)
    slot_ids = jnp.arange(BCAP, dtype=jnp.int32)
    wanted = jnp.sum(
        jnp.where(present[:, None, :] & (rank[:, None, :] == slot_ids[:, None]), local_ids, 0),
        axis=2,
    )
    chosen = select_blocks(wanted.reshape(span * BCAP), packed, 16)
    replies = lax.all_to_all(
        chosen.reshape(span, BCAP * block_rows, lanes),
        "nodes",
        split_axis=0,
        concat_axis=0,
        tiled=True,
    ).reshape(span * BCAP, block_rows, lanes)

    extra = jnp.concatenate(
        [
            left,
            right,
            heard[:, 2 : 2 + features // lanes].reshape(span, features),
            jnp.zeros((block_rows - span, features), bf16),
        ],
        axis=0,
    )
    _, extra_packed = project(extra, project_weight, extra.shape[0])
    global_ids = me * blocks + local_ids
    shift = jnp.mod(neigh_source - global_ids[:, None] + 1, all_blocks) + local_ids[:, None]
    near_sum, near_total = near_terms(
        shift.reshape(-1),
        neigh_count.reshape(-1),
        query,
        packed,
        extra_packed[0],
        extra_packed[1],
        extra_packed[2],
        neigh_rows,
        4,
    )

    own_present = jnp.any(
        source[0][:, None] == jnp.arange(all_blocks, dtype=jnp.int32), axis=0
    ).reshape(span, blocks)
    own_rank = ranked_blocks(own_present).reshape(1, all_blocks)
    tile_rank = jnp.sum(
        jnp.where(source[0][:, None] == jnp.arange(all_blocks, dtype=jnp.int32), own_rank, 0), axis=1
    )
    slots = owner[0] * BCAP + tile_rank
    attended = far_terms(
        slots,
        expander_count.reshape(-1),
        query,
        replies,
        expander_rows,
        near_sum,
        near_total,
        shares,
        4,
    )
    regrouped = lax.all_to_all(attended, "heads", split_axis=0, concat_axis=0, tiled=True)
    return tail(
        share.reshape(1),
        regrouped,
        node_states,
        output_weight,
        expand,
        expand_bias.reshape(shares, 1, -1),
        contract,
    )


def solution(mesh):
    return jax.shard_map(
        local,
        mesh=mesh,
        in_specs=(
            P("nodes", None),
            P("nodes", None),
            P(None, "heads"),
            P(),
            P(None, "heads"),
            P(),
            P("heads", None),
            P("nodes", None),
            P("nodes", None, None),
            P("nodes", None),
            P("nodes", None),
            P("nodes", None, None),
            P("nodes", None),
        ),
        out_specs=P(("nodes", "heads"), None),
        check_vma=False,
    )
```

```python
import functools

import jax
import jax.numpy as jnp
from jax import lax
from jax.experimental import pallas as pl
from jax.experimental.pallas import tpu as pltpu
from jax.sharding import PartitionSpec as P

HEAD_DIM = 64
BCAP = 4

eps_norm = 1e-05
clip_level = 5.0
TAIL = 10
TIGHT = 58

f32 = jnp.float32
bf16 = jnp.bfloat16
def params(mib):
    return pltpu.CompilerParams(vmem_limit_bytes=mib * 2**20)


def layer_norm(values):
    values = values.astype(f32)
    center = values - jnp.mean(values, axis=-1, keepdims=True)
    spread = jnp.mean(center * center, axis=-1, keepdims=True)
    return center * lax.rsqrt(spread + eps_norm)


vmem = pl.BlockSpec(memory_space=pltpu.VMEM)
smem = pl.BlockSpec(memory_space=pltpu.SMEM)


def ask_kernel(source_ref, virtual_ref, out_ref, slot_ref, table_ref):
    tiles, blocks = source_ref.shape
    span, _, lanes = out_ref.shape
    bits = blocks.bit_length() - 1
    source = jnp.concatenate([source_ref[t : t + 1, :] for t in range(tiles)], axis=1)
    across = jnp.broadcast_to(source, (lanes, lanes))
    down = across.T
    up = lax.broadcasted_iota(jnp.int32, (lanes, lanes), 0)
    along = lax.broadcasted_iota(jnp.int32, (lanes, lanes), 1)
    again = jnp.where((across == down) & (along < up), 1.0, 0.0)
    first = jnp.sum(again, axis=1, keepdims=True) == 0.0
    same = lax.shift_right_logical(across, bits) == lax.shift_right_logical(down, bits)
    below = jnp.where(same & (down < across) & first, 1.0, 0.0)
    rank = jnp.sum(below, axis=0, keepdims=True).astype(jnp.int32)
    slot = lax.shift_right_logical(source, bits) * BCAP + rank
    slot_ref[...] = slot
    slot_down = jnp.broadcast_to(slot, (lanes, lanes)).T
    place = jnp.where((slot_down == along) & first, (down & (blocks - 1)).astype(f32), 0.0)
    table_ref[...] = jnp.zeros_like(table_ref)
    table_ref[0:1, :] = jnp.sum(place, axis=0, keepdims=True)
    for part in range(virtual_ref.shape[1] // lanes):
        table_ref[8 + part : 9 + part, :] = virtual_ref[
            :, part * lanes : (part + 1) * lanes
        ].astype(f32)
    table = table_ref[...].astype(bf16)
    for item in range(span):
        out_ref[item] = table


def ask(source, virtual_states, span):
    lanes = 128
    return pl.pallas_call(
        ask_kernel,
        in_specs=[vmem, vmem],
        out_specs=[vmem, vmem],
        out_shape=[
            jax.ShapeDtypeStruct((span, 16, lanes), bf16),
            jax.ShapeDtypeStruct((1, lanes), jnp.int32),
        ],
        scratch_shapes=[pltpu.VMEM((16, lanes), f32)],
        compiler_params=params(56),
        name="ask",
    )(source, virtual_states)


def project_kernel(x_ref, w_ref, query_ref, pack_ref):
    head = HEAD_DIM
    wide = 2 * head
    rows = min(x_ref.shape[0], 512)
    for start in range(0, x_ref.shape[0], rows):
        normed = layer_norm(x_ref[start : start + rows, :]).astype(bf16)
        sides = lax.dot_general(
            w_ref[...], normed, (((1,), (1,)), ((), ())), preferred_element_type=f32
        ).astype(bf16)
        query_ref[:, start : start + rows] = sides[:head] * jnp.asarray(head**-0.5, bf16)
        for item in range(rows // wide):
            pack_ref[start // wide + item] = sides[head:, item * wide : (item + 1) * wide]


def project(states, weight_t, step_rows, mib):
    rows, features = states.shape
    wide = 2 * HEAD_DIM
    return pl.pallas_call(
        project_kernel,
        grid=(rows // step_rows,),
        in_specs=[
            pl.BlockSpec((step_rows, features), lambda i: (i, 0)),
            pl.BlockSpec(weight_t.shape, lambda i: (0, 0)),
        ],
        out_specs=[
            pl.BlockSpec((HEAD_DIM, step_rows), lambda i: (0, i)),
            pl.BlockSpec((step_rows // wide, wide, wide), lambda i: (i, 0, 0)),
        ],
        out_shape=[
            jax.ShapeDtypeStruct((HEAD_DIM, rows), bf16),
            jax.ShapeDtypeStruct((rows // wide, wide, wide), bf16),
        ],
        compiler_params=params(mib),
        name="project",
    )(states, weight_t)


def select_kernel(
    me_ref, heard_ref, pack_ref, out_ref, heard_buf, pack_buf, table_ref, place_ref, copy_sem, sems
):
    span = heard_ref.shape[0]
    fetch_pack = pltpu.make_async_copy(pack_ref, pack_buf, sems.at[0])
    fetch_heard = pltpu.make_async_copy(heard_ref, heard_buf, sems.at[1])
    fetch_heard.start()
    fetch_pack.start()
    fetch_heard.wait()
    table_ref[...] = heard_buf[:, 0, :].astype(f32).astype(jnp.int32)
    fetch_place = pltpu.make_async_copy(table_ref, place_ref, sems.at[2])
    fetch_place.start()
    fetch_place.wait()
    fetch_pack.wait()
    base = me_ref[0] * BCAP

    def send(item, _):
        for slot in range(BCAP):
            pltpu.make_async_copy(
                pack_buf.at[place_ref[item, base + slot]],
                out_ref.at[item * BCAP + slot],
                copy_sem,
            ).start()
        return 0

    lax.fori_loop(0, span, send, 0, unroll=2)
    pltpu.make_async_copy(out_ref, out_ref, copy_sem).wait()


def select_blocks(me, heard, packed):
    span, _, lanes = heard.shape
    anywhere = pl.BlockSpec(memory_space=pl.ANY)
    return pl.pallas_call(
        select_kernel,
        in_specs=[smem, anywhere, anywhere],
        out_specs=anywhere,
        out_shape=jax.ShapeDtypeStruct((span * BCAP,) + packed.shape[1:], bf16),
        scratch_shapes=[
            pltpu.VMEM(heard.shape, bf16),
            pltpu.VMEM(packed.shape, bf16),
            pltpu.VMEM((span, lanes), jnp.int32),
            pltpu.SMEM((span, lanes), jnp.int32),
            pltpu.SemaphoreType.DMA,
            pltpu.SemaphoreType.DMA((3,)),
        ],
        compiler_params=params(TIGHT),
        name="select_blocks",
    )(me, heard, packed)


def tile_terms(query, blocks, rows, counts):
    head = HEAD_DIM
    wide = 2 * head
    lane = lax.broadcasted_iota(jnp.int32, (1, wide), 1)
    spot = lax.broadcasted_iota(jnp.int32, (wide, wide), 0)
    summed, total = None, None
    for block, row, count in zip(blocks, rows, counts):
        pick = jnp.where(spot == row, 1.0, 0.0).astype(bf16)
        pairs = jnp.dot(block, pick, preferred_element_type=f32)
        score = jnp.sum(pairs[:head] * query, axis=0, keepdims=True)
        weight = jnp.exp(jnp.clip(score, -clip_level, clip_level))
        weight = jnp.where(lane < count, weight, 0.0)
        value = pairs[head:] * weight
        summed = value if summed is None else summed + value
        total = weight if total is None else total + weight
    return summed, total


def tile_rows(rows_ref, block):
    rows = rows_ref[block]
    return [rows[tile : tile + 1] for tile in range(rows.shape[0])]


def near_kernel(
    group, place_ref, count_ref, query_ref, pack_ref, virtual_ref, rows_ref, sum_ref, total_ref
):
    head = HEAD_DIM
    blocks, tiles, wide = rows_ref.shape
    virtual_total = 32
    virtual_keys = virtual_ref[0, :head, :].T[:virtual_total]
    virtual_values = virtual_ref[0, head:, :virtual_total]

    def step(turn, _):
        for item in range(group):
            block = turn * group + item
            lanes = pl.ds(pl.multiple_of(block * wide, wide), wide)
            query = query_ref[:, lanes]
            tile_blocks = [pack_ref[place_ref[block * tiles + t]] for t in range(tiles)]
            counts = [count_ref[block * tiles + t] for t in range(tiles)]
            summed, total = tile_terms(
                query.astype(f32), tile_blocks, tile_rows(rows_ref, block), counts
            )
            scores = jnp.dot(virtual_keys, query, preferred_element_type=f32)
            weights = jnp.exp(jnp.clip(scores, -clip_level, clip_level))
            total = total + jnp.sum(weights, axis=0, keepdims=True)
            summed = summed + jnp.dot(
                virtual_values, weights.astype(bf16), preferred_element_type=f32
            )
            sum_ref[:, lanes] = summed
            total_ref[:, lanes] = total
        return 0

    lax.fori_loop(0, blocks // group, step, 0)


def near_terms(places, counts, query, packed, virtual, rows, group):
    head, total = query.shape
    return pl.pallas_call(
        functools.partial(near_kernel, group),
        in_specs=[smem, smem] + [vmem] * 4,
        out_specs=[vmem, vmem],
        out_shape=[
            jax.ShapeDtypeStruct((head, total), f32),
            jax.ShapeDtypeStruct((1, total), f32),
        ],
        compiler_params=params(TIGHT),
        cost_estimate=pl.CostEstimate(
            flops=8 * 2**30, bytes_accessed=4 * 2**20, transcendentals=2**20
        ),
        name="near_terms",
    )(places, counts, query, packed, virtual, rows)


def far_kernel(
    group, slot_ref, count_ref, edge_ref, query_ref, reply_ref, rows_ref, left_ref, right_ref,
    edge_rows_ref, sum_ref, total_ref, out_ref,
):
    blocks, tiles, wide = rows_ref.shape
    share_blocks = blocks // out_ref.shape[0]

    def one(block, more_blocks=(), more_rows=(), more_counts=()):
        lanes = pl.ds(pl.multiple_of(block * wide, wide), wide)
        tile_blocks = [reply_ref[slot_ref[0, t * blocks + block]] for t in range(tiles)]
        counts = [count_ref[block * tiles + t] for t in range(tiles)]
        summed, total = tile_terms(
            query_ref[:, lanes].astype(f32),
            tile_blocks + list(more_blocks),
            tile_rows(rows_ref, block) + list(more_rows),
            counts + list(more_counts),
        )
        total = total + total_ref[:, lanes]
        result = (summed + sum_ref[:, lanes]) * (1.0 / total)
        inner = pl.ds(pl.multiple_of(lax.rem(block, share_blocks) * wide, wide), wide)
        out_ref[lax.div(block, share_blocks), :, inner] = result.astype(bf16)

    near_tiles = edge_rows_ref.shape[1]
    for end, halo_ref in enumerate((left_ref, right_ref)):
        one(
            jnp.int32(end * (blocks - 1)),
            [halo_ref[0]] * near_tiles,
            tile_rows(edge_rows_ref, end),
            [edge_ref[end * near_tiles + t] for t in range(near_tiles)],
        )

    def step(turn, _):
        for item in range(group):
            one(1 + turn * group + item)
        return 0

    lax.fori_loop(0, (blocks - 2) // group, step, 0)


def far_terms(
    slots, counts, edges, query, replies, rows, left, right, edge_rows, near_sum, near_total, shares,
    group,
):
    head, total = query.shape
    return pl.pallas_call(
        functools.partial(far_kernel, group),
        in_specs=[smem] * 3 + [vmem] * 8,
        out_specs=vmem,
        out_shape=jax.ShapeDtypeStruct((shares, head, total // shares), bf16),
        compiler_params=params(TIGHT),
        name="far_terms",
    )(slots, counts, edges, query, replies, rows, left, right, edge_rows, near_sum, near_total)


def piece_kernel(core_ref, expand_ref, contract_ref, out_ref):
    wide = out_ref.shape[0] // 2
    for core in range(2):

        @pl.when(core_ref[0] == core)
        def _():
            span = slice(core * wide, (core + 1) * wide)
            out_ref[:wide] = expand_ref[:, span].T
            out_ref[wide:] = contract_ref[span, :]


def weight_piece(core, expand, contract):
    features, width = expand.shape
    return pl.pallas_call(
        piece_kernel,
        in_specs=[smem, vmem, vmem],
        out_specs=vmem,
        out_shape=jax.ShapeDtypeStruct((width, features), bf16),
        compiler_params=params(16),
        name="weight_piece",
    )(core, expand, contract)


def tail_kernel(
    offsets, place_ref, att_ref, own_ref, output_ref, mine_ref, theirs_ref, bias_ref, out_ref
):
    heads, head, rows = att_ref.shape
    features = heads * head
    parts = len(offsets)
    wide = mine_ref.shape[1] // 2
    attended = att_ref[...].reshape(features, rows).T
    residual = own_ref[...].astype(f32) + jnp.dot(
        attended, output_ref[...], preferred_element_type=f32
    )
    normed = layer_norm(residual).astype(bf16)
    summed = residual
    for part, offset in enumerate(offsets):
        owner = lax.rem(place_ref[0] + offset + parts, parts)
        bias = jnp.concatenate(
            [bias_ref[2 * owner + place_ref[1]], bias_ref[2 * owner + 1 - place_ref[1]]], axis=1
        )
        first = jnp.concatenate([mine_ref[part, :wide], theirs_ref[part, :wide]], axis=0)
        second = jnp.concatenate([mine_ref[part, wide:], theirs_ref[part, wide:]], axis=0)
        inner = lax.dot_general(
            normed, first, (((1,), (1,)), ((), ())), preferred_element_type=f32
        )
        inner = inner + bias
        hidden = ((inner * 0.5) * (1.0 + lax.erf(inner * (0.5**0.5)))).astype(bf16)
        summed = summed + jnp.dot(hidden, second, preferred_element_type=f32)
    out_ref[...] = summed.astype(bf16)


def tail(place, regrouped, own, output_weight, mine, theirs, bias, offsets):
    return pl.pallas_call(
        functools.partial(tail_kernel, offsets),
        in_specs=[smem] + [vmem] * 6,
        out_specs=vmem,
        out_shape=jax.ShapeDtypeStruct(own.shape, bf16),
        compiler_params=params(TAIL),
        name="tail",
    )(place, regrouped, own, output_weight, mine, theirs, bias)


def local(
    node_states,
    virtual_states,
    project_weight,
    output_weight,
    expand_weight,
    expand_bias,
    contract_weight,
    neigh_source,
    neigh_rows,
    neigh_count,
    expander_source,
    expander_rows,
    expander_count,
):
    span = lax.axis_size("nodes")
    me = lax.axis_index("nodes").astype(jnp.int32)
    shares = lax.axis_size("heads")
    share = lax.axis_index("heads").astype(jnp.int32)
    core = jnp.bitwise_and(me, 1)
    blocks, neigh_tiles, block_rows = neigh_rows.shape
    rows, features = node_states.shape
    all_blocks = blocks * span
    lanes = 128
    barrier = lax.optimization_barrier

    message, slots = ask(expander_source.T, virtual_states, span)
    heard = lax.all_to_all(message, "nodes", split_axis=0, concat_axis=0, tiled=True)
    weight_t = project_weight.T
    query, packed = project(node_states, weight_t, rows // 2, TIGHT)
    chosen = select_blocks(me.reshape(1), heard, packed)
    replies = lax.all_to_all(
        chosen.reshape(span, BCAP * block_rows, lanes),
        "nodes",
        split_axis=0,
        concat_axis=0,
        tiled=True,
    ).reshape(span * BCAP, block_rows, lanes)

    heard, chosen = barrier((heard, chosen))
    extra = jnp.concatenate(
        [
            heard[:, 8 : 8 + features // lanes].reshape(span, features),
            jnp.zeros((block_rows - span, features), bf16),
        ],
        axis=0,
    )
    _, virtual_packed = project(extra, weight_t, extra.shape[0], 16)
    local_ids = jnp.arange(blocks, dtype=jnp.int32)[:, None]
    global_ids = me * blocks + local_ids
    place = jnp.mod(neigh_source - global_ids + 1, all_blocks) + local_ids - 1
    inside = (place >= 0) & (place < blocks)
    near_count = jnp.where(inside, neigh_count, 0)
    edge_count = jnp.where(inside, 0, neigh_count)
    near_sum, near_total = near_terms(
        jnp.clip(place, 0, blocks - 1).reshape(-1),
        near_count.reshape(-1),
        query,
        packed,
        virtual_packed,
        neigh_rows,
        4,
    )

    half = expand_weight.shape[1] // 2
    piece = weight_piece(core.reshape(1), expand_weight, contract_weight)
    piece, virtual_packed = barrier((piece, virtual_packed))
    upward = [(i, (i + 1) % shares) for i in range(shares)]
    downward = [((i + 1) % shares, i) for i in range(shares)]
    pieces, offsets = [piece], [0]
    above, below = piece, piece
    for step in range(1, shares // 2 + 1):
        below = lax.ppermute(below, "heads", upward)
        if step == 1:
            below, near_total = barrier((below, near_total))
        pieces.append(below)
        offsets.append(-step)
        if step < shares // 2:
            above = lax.ppermute(above, "heads", downward)
            pieces.append(above)
            offsets.append(step)
    mine = jnp.stack(pieces)
    theirs = lax.ppermute(mine, "nodes", [(i, i ^ 1) for i in range(span)])

    first_block, last_block, virtual_packed = barrier((packed[:1], packed[-1:], virtual_packed))
    left = lax.ppermute(last_block, "nodes", [(i, (i + 1) % span) for i in range(span)])
    right = lax.ppermute(first_block, "nodes", [((i + 1) % span, i) for i in range(span)])

    edge_rows = jnp.concatenate([neigh_rows[:1], neigh_rows[-1:]], axis=0)
    attended = far_terms(
        slots,
        expander_count.reshape(-1),
        jnp.concatenate([edge_count[0], edge_count[-1]]),
        query,
        replies,
        expander_rows,
        left,
        right,
        edge_rows,
        near_sum,
        near_total,
        shares,
        10,
    )
    own = lax.dynamic_slice_in_dim(node_states, share * (rows // shares), rows // shares, 0)
    attended, own, mine = barrier((attended, own, mine))
    regrouped = lax.all_to_all(attended, "heads", split_axis=0, concat_axis=0, tiled=True)
    return tail(
        jnp.stack([share, core]),
        regrouped,
        own,
        output_weight,
        mine,
        theirs,
        expand_bias.reshape(2 * shares, 1, half),
        tuple(offsets),
    )


def solution(mesh):
    return jax.shard_map(
        local,
        mesh=mesh,
        in_specs=(
            P("nodes", None),
            P("nodes", None),
            P(None, "heads"),
            P(),
            P(None, "heads"),
            P(),
            P("heads", None),
            P("nodes", None),
            P("nodes", None, None),
            P("nodes", None),
            P("nodes", None),
            P("nodes", None, None),
            P("nodes", None),
        ),
        out_specs=P(("nodes", "heads"), None),
        check_vma=False,
    )
```

```python
import functools

import jax
import jax.numpy as jnp
from jax import lax
from jax.experimental import pallas as pl
from jax.experimental.pallas import tpu as pltpu
from jax.sharding import PartitionSpec as P

HEAD_DIM = 64
BCAP = 4

eps_norm = 1e-05
clip_level = 5.0
TAIL = 10
STAGE = 16
SELECT = 52
TIGHT = 58

f32 = jnp.float32
bf16 = jnp.bfloat16
def params(mib):
    return pltpu.CompilerParams(vmem_limit_bytes=mib * 2**20)


def layer_norm(values):
    values = values.astype(f32)
    center = values - jnp.mean(values, axis=-1, keepdims=True)
    spread = jnp.mean(center * center, axis=-1, keepdims=True)
    return center * lax.rsqrt(spread + eps_norm)


vmem = pl.BlockSpec(memory_space=pltpu.VMEM)
smem = pl.BlockSpec(memory_space=pltpu.SMEM)


def ask_kernel(source_ref, virtual_ref, out_ref, slot_ref, table_ref):
    tiles, blocks = source_ref.shape
    span, _, lanes = out_ref.shape
    bits = blocks.bit_length() - 1
    source = jnp.concatenate([source_ref[t : t + 1, :] for t in range(tiles)], axis=1)
    across = jnp.broadcast_to(source, (lanes, lanes))
    down = across.T
    up = lax.broadcasted_iota(jnp.int32, (lanes, lanes), 0)
    along = lax.broadcasted_iota(jnp.int32, (lanes, lanes), 1)
    again = jnp.where((across == down) & (along < up), 1.0, 0.0)
    first = jnp.sum(again, axis=1, keepdims=True) == 0.0
    same = lax.shift_right_logical(across, bits) == lax.shift_right_logical(down, bits)
    below = jnp.where(same & (down < across) & first, 1.0, 0.0)
    rank = jnp.sum(below, axis=0, keepdims=True).astype(jnp.int32)
    slot = lax.shift_right_logical(source, bits) * BCAP + rank
    slot_ref[...] = slot
    slot_down = jnp.broadcast_to(slot, (lanes, lanes)).T
    place = jnp.where((slot_down == along) & first, (down & (blocks - 1)).astype(f32), 0.0)
    table_ref[...] = jnp.zeros_like(table_ref)
    table_ref[0:1, :] = jnp.sum(place, axis=0, keepdims=True)
    for part in range(virtual_ref.shape[1] // lanes):
        table_ref[8 + part : 9 + part, :] = virtual_ref[
            :, part * lanes : (part + 1) * lanes
        ].astype(f32)
    table = table_ref[...].astype(bf16)
    for item in range(span):
        out_ref[item] = table


def ask(source, virtual_states, span):
    lanes = 128
    return pl.pallas_call(
        ask_kernel,
        in_specs=[vmem, vmem],
        out_specs=[vmem, vmem],
        out_shape=[
            jax.ShapeDtypeStruct((span, 16, lanes), bf16),
            jax.ShapeDtypeStruct((1, lanes), jnp.int32),
        ],
        scratch_shapes=[pltpu.VMEM((16, lanes), f32)],
        compiler_params=params(56),
        name="ask",
    )(source, virtual_states)


def project_kernel(core_ref, x_ref, w_ref, *refs):
    query_ref, pack_ref = refs[2:4] if len(refs) > 2 else refs
    rest = refs
    head = HEAD_DIM
    wide = 2 * head
    rows = min(x_ref.shape[0], 512)
    for start in range(0, x_ref.shape[0], rows):
        normed = layer_norm(x_ref[start : start + rows, :]).astype(bf16)
        sides = lax.dot_general(
            w_ref[...], normed, (((1,), (1,)), ((), ())), preferred_element_type=f32
        ).astype(bf16)
        query_ref[:, start : start + rows] = sides[:head] * jnp.asarray(head**-0.5, bf16)
        for item in range(rows // wide):
            pack_ref[start // wide + item] = sides[head:, item * wide : (item + 1) * wide]
    if len(rest) > 2:
        expand_ref, contract_ref, _, _, outer_ref, inner_ref, piece_ref = rest
        first = pl.program_id(0) == 0
        last = pl.program_id(0) == pl.num_programs(0) - 1
        even = core_ref[0] == 0
        units = piece_ref.shape[0] // 2
        for core in range(2):

            @pl.when(first & (core_ref[0] == core))
            def _():
                span = slice(core * units, (core + 1) * units)
                piece_ref[:units] = expand_ref[:, span].T
                piece_ref[units:] = contract_ref[span, :]

        @pl.when(first & even)
        def _():
            outer_ref[0] = pack_ref[0]

        @pl.when(first & jnp.logical_not(even))
        def _():
            inner_ref[0] = pack_ref[0]

        @pl.when(last & even)
        def _():
            inner_ref[0] = pack_ref[pack_ref.shape[0] - 1]

        @pl.when(last & jnp.logical_not(even))
        def _():
            outer_ref[0] = pack_ref[pack_ref.shape[0] - 1]


def project(core, states, weight_t, step_rows, mib, *feed):
    rows, features = states.shape
    wide = 2 * HEAD_DIM
    whole = [pl.BlockSpec(array.shape, lambda i: (0, 0)) for array in feed]
    more_specs, more_shapes = [], []
    if feed:
        more_specs = [pl.BlockSpec((1, wide, wide), lambda i: (0, 0, 0))] * 2
        more_specs.append(pl.BlockSpec((wide * 2, features), lambda i: (0, 0)))
        more_shapes = [jax.ShapeDtypeStruct((1, wide, wide), bf16)] * 2
        more_shapes.append(jax.ShapeDtypeStruct((wide * 2, features), bf16))
    return pl.pallas_call(
        project_kernel,
        grid=(rows // step_rows,),
        in_specs=[
            smem,
            pl.BlockSpec((step_rows, features), lambda i: (i, 0)),
            pl.BlockSpec(weight_t.shape, lambda i: (0, 0)),
        ]
        + whole,
        out_specs=[
            pl.BlockSpec((HEAD_DIM, step_rows), lambda i: (0, i)),
            pl.BlockSpec((step_rows // wide, wide, wide), lambda i: (i, 0, 0)),
        ]
        + more_specs,
        out_shape=[
            jax.ShapeDtypeStruct((HEAD_DIM, rows), bf16),
            jax.ShapeDtypeStruct((rows // wide, wide, wide), bf16),
        ]
        + more_shapes,
        compiler_params=params(mib),
        name="project",
    )(core, states, weight_t, *feed)


def select_kernel(
    me_ref, heard_ref, pack_ref, out_ref, heard_buf, pack_buf, table_ref, place_ref, copy_sem, sems
):
    span = heard_ref.shape[0]
    fetch_pack = pltpu.make_async_copy(pack_ref, pack_buf, sems.at[0])
    fetch_heard = pltpu.make_async_copy(heard_ref, heard_buf, sems.at[1])
    fetch_heard.start()
    fetch_pack.start()
    fetch_heard.wait()
    table_ref[...] = heard_buf[:, 0, :].astype(f32).astype(jnp.int32)
    fetch_place = pltpu.make_async_copy(table_ref, place_ref, sems.at[2])
    fetch_place.start()
    fetch_place.wait()
    fetch_pack.wait()
    base = me_ref[0] * BCAP

    def send(item, _):
        for slot in range(BCAP):
            pltpu.make_async_copy(
                pack_buf.at[place_ref[item, base + slot]],
                out_ref.at[item * BCAP + slot],
                copy_sem,
            ).start()
        return 0

    lax.fori_loop(0, span, send, 0, unroll=2)
    pltpu.make_async_copy(out_ref, out_ref, copy_sem).wait()


def select_blocks(me, heard, packed):
    span, _, lanes = heard.shape
    anywhere = pl.BlockSpec(memory_space=pl.ANY)
    return pl.pallas_call(
        select_kernel,
        in_specs=[smem, anywhere, anywhere],
        out_specs=anywhere,
        out_shape=jax.ShapeDtypeStruct((span * BCAP,) + packed.shape[1:], bf16),
        scratch_shapes=[
            pltpu.VMEM(heard.shape, bf16),
            pltpu.VMEM(packed.shape, bf16),
            pltpu.VMEM((span, lanes), jnp.int32),
            pltpu.SMEM((span, lanes), jnp.int32),
            pltpu.SemaphoreType.DMA,
            pltpu.SemaphoreType.DMA((3,)),
        ],
        compiler_params=params(SELECT),
        name="select_blocks",
    )(me, heard, packed)


def tile_terms(query, blocks, rows, counts):
    head = HEAD_DIM
    wide = 2 * head
    lane = lax.broadcasted_iota(jnp.int32, (1, wide), 1)
    spot = lax.broadcasted_iota(jnp.int32, (wide, wide), 0)
    summed, total = None, None
    for block, row, count in zip(blocks, rows, counts):
        pick = jnp.where(spot == row, 1.0, 0.0).astype(bf16)
        pairs = jnp.dot(block, pick, preferred_element_type=f32)
        score = jnp.sum(pairs[:head] * query, axis=0, keepdims=True)
        weight = jnp.exp(jnp.clip(score, -clip_level, clip_level))
        weight = jnp.where(lane < count, weight, 0.0)
        value = pairs[head:] * weight
        summed = value if summed is None else summed + value
        total = weight if total is None else total + weight
    return summed, total


def tile_rows(rows_ref, block):
    rows = rows_ref[block]
    return [rows[tile : tile + 1] for tile in range(rows.shape[0])]


def near_kernel(
    group, place_ref, count_ref, query_ref, pack_ref, inner_ref, virtual_ref, rows_ref, sum_ref,
    total_ref, window_ref,
):
    head = HEAD_DIM
    blocks, tiles, wide = rows_ref.shape
    virtual_total = 32
    virtual_keys = virtual_ref[0, :head, :].T[:virtual_total]
    virtual_values = virtual_ref[0, head:, :virtual_total]
    window_ref[blocks] = inner_ref[0]

    def fill(block, _):
        window_ref[block] = pack_ref[block]
        return 0

    lax.fori_loop(0, blocks, fill, 0, unroll=8)

    def step(turn, _):
        for item in range(group):
            block = turn * group + item
            lanes = pl.ds(pl.multiple_of(block * wide, wide), wide)
            query = query_ref[:, lanes]
            tile_blocks = [window_ref[place_ref[block * tiles + t]] for t in range(tiles)]
            counts = [count_ref[block * tiles + t] for t in range(tiles)]
            summed, total = tile_terms(
                query.astype(f32), tile_blocks, tile_rows(rows_ref, block), counts
            )
            scores = jnp.dot(virtual_keys, query, preferred_element_type=f32)
            weights = jnp.exp(jnp.clip(scores, -clip_level, clip_level))
            total = total + jnp.sum(weights, axis=0, keepdims=True)
            summed = summed + jnp.dot(
                virtual_values, weights.astype(bf16), preferred_element_type=f32
            )
            sum_ref[:, lanes] = summed
            total_ref[:, lanes] = total
        return 0

    lax.fori_loop(0, blocks // group, step, 0)


def near_terms(places, counts, query, packed, inner, virtual, rows, group):
    head, total = query.shape
    blocks = packed.shape[0]
    return pl.pallas_call(
        functools.partial(near_kernel, group),
        in_specs=[smem, smem] + [vmem] * 5,
        out_specs=[vmem, vmem],
        out_shape=[
            jax.ShapeDtypeStruct((head, total), f32),
            jax.ShapeDtypeStruct((1, total), f32),
        ],
        scratch_shapes=[pltpu.VMEM((blocks + 1,) + packed.shape[1:], bf16)],
        compiler_params=params(TIGHT),
        cost_estimate=pl.CostEstimate(flops=1, bytes_accessed=1, transcendentals=0),
        name="near_terms",
    )(places, counts, query, packed, inner, virtual, rows)


def far_kernel(
    group, share_ref, slot_ref, count_ref, edge_ref, edge_count_ref, query_ref, reply_ref, rows_ref,
    outer_ref, edge_rows_ref, sum_ref, total_ref, *rest
):
    outs, (out_ref, sem) = rest[:-2], rest[-2:]
    blocks, tiles, wide = rows_ref.shape
    share_blocks = blocks // out_ref.shape[0]
    edge = edge_ref[0]
    near_tiles = edge_rows_ref.shape[1]
    edge_sum, edge_total = tile_terms(
        query_ref[:, pl.ds(pl.multiple_of(edge * wide, wide), wide)].astype(f32),
        [outer_ref[0]] * near_tiles,
        tile_rows(edge_rows_ref, edge),
        [edge_count_ref[edge * near_tiles + t] for t in range(near_tiles)],
    )

    def step(turn, _):
        for item in range(group):
            block = turn * group + item
            lanes = pl.ds(pl.multiple_of(block * wide, wide), wide)
            tile_blocks = [reply_ref[slot_ref[0, t * blocks + block]] for t in range(tiles)]
            counts = [count_ref[block * tiles + t] for t in range(tiles)]
            summed, total = tile_terms(
                query_ref[:, lanes].astype(f32), tile_blocks, tile_rows(rows_ref, block), counts
            )
            here = (block == edge).astype(f32)
            total = total + total_ref[:, lanes] + here * edge_total
            result = (summed + sum_ref[:, lanes] + here * edge_sum) * (1.0 / total)
            inner = pl.ds(pl.multiple_of(lax.rem(block, share_blocks) * wide, wide), wide)
            out_ref[lax.div(block, share_blocks), :, inner] = result.astype(bf16)
        return 0

    lax.fori_loop(0, blocks // group, step, 0)
    copies = []
    for ahead, out in enumerate(outs):
        share = lax.rem(share_ref[0] + ahead, len(outs))
        copies.append(pltpu.make_async_copy(out_ref.at[share], out, sem.at[ahead]))
        copies[-1].start()
    for copy in copies:
        copy.wait()


def far_terms(
    share, slots, counts, edge, edge_counts, query, replies, rows, outer, edge_rows, near_sum,
    near_total, shares, group,
):
    head, total = query.shape
    return pl.pallas_call(
        functools.partial(far_kernel, group),
        in_specs=[smem] * 5 + [vmem] * 7,
        out_specs=[pl.BlockSpec(memory_space=pl.ANY)] * shares,
        out_shape=[jax.ShapeDtypeStruct((head, total // shares), bf16)] * shares,
        scratch_shapes=[
            pltpu.VMEM((shares, head, total // shares), bf16),
            pltpu.SemaphoreType.DMA((shares,)),
        ],
        compiler_params=params(TIGHT),
        name="far_terms",
    )(
        share, slots, counts, edge, edge_counts, query, replies, rows, outer, edge_rows, near_sum,
        near_total,
    )


def stage_kernel(share_ref, states_ref, *refs):
    sources, (own_ref, *copies, sems) = refs[:3], refs[3:]
    rows = own_ref.shape[0]
    start = pl.multiple_of(share_ref[0] * rows, rows)
    fetches = [pltpu.make_async_copy(states_ref.at[pl.ds(start, rows)], own_ref, sems.at[0])]
    for item, (source, copy) in enumerate(zip(sources, copies)):
        fetches.append(pltpu.make_async_copy(source, copy, sems.at[item + 1]))
    for fetch in fetches:
        fetch.start()
    for fetch in fetches:
        fetch.wait()


def stage(share, states, rows, *others):
    return pl.pallas_call(
        stage_kernel,
        in_specs=[smem] + [pl.BlockSpec(memory_space=pl.ANY)] * (1 + len(others)),
        out_specs=[vmem] * (1 + len(others)),
        out_shape=[jax.ShapeDtypeStruct((rows, states.shape[1]), bf16)]
        + [jax.ShapeDtypeStruct(other.shape, bf16) for other in others],
        scratch_shapes=[pltpu.SemaphoreType.DMA((1 + len(others),))],
        compiler_params=params(STAGE),
        name="stage",
    )(share, states, *others)


def tail_kernel(
    offsets, place_ref, own_ref, output_ref, mine_ref, theirs_ref, bias_ref, *rest
):
    pieces, (out_ref, att_ref) = rest[:-2], rest[-2:]
    features, rows = att_ref.shape
    head, _ = pieces[0].shape
    for behind, piece in enumerate(pieces):
        owner = lax.rem(place_ref[0] + len(pieces) - behind, len(pieces))
        att_ref[pl.ds(pl.multiple_of(owner * head, head), head), :] = piece[...]
    parts = len(offsets)
    wide = mine_ref.shape[1] // 2
    attended = att_ref[...].T
    residual = own_ref[...].astype(f32) + jnp.dot(
        attended, output_ref[...], preferred_element_type=f32
    )
    normed = layer_norm(residual).astype(bf16)
    summed = residual
    for part, offset in enumerate(offsets):
        owner = lax.rem(place_ref[0] + offset + parts, parts)
        bias = jnp.concatenate(
            [bias_ref[2 * owner + place_ref[1]], bias_ref[2 * owner + 1 - place_ref[1]]], axis=1
        )
        first = jnp.concatenate([mine_ref[part, :wide], theirs_ref[part, :wide]], axis=0)
        second = jnp.concatenate([mine_ref[part, wide:], theirs_ref[part, wide:]], axis=0)
        inner = lax.dot_general(
            normed, first, (((1,), (1,)), ((), ())), preferred_element_type=f32
        )
        inner = inner + bias
        hidden = ((inner * 0.5) * (1.0 + lax.erf(inner * (0.5**0.5)))).astype(bf16)
        summed = summed + jnp.dot(hidden, second, preferred_element_type=f32)
    out_ref[...] = summed.astype(bf16)


def tail(place, own, output_weight, mine, theirs, bias, pieces, offsets):
    rows, features = own.shape
    return pl.pallas_call(
        functools.partial(tail_kernel, offsets),
        in_specs=[smem] + [vmem] * (5 + len(pieces)),
        out_specs=vmem,
        out_shape=jax.ShapeDtypeStruct(own.shape, bf16),
        scratch_shapes=[pltpu.VMEM((features, rows), bf16)],
        compiler_params=params(TAIL),
        name="tail",
    )(place, own, output_weight, mine, theirs, bias, *pieces)


def local(
    node_states,
    virtual_states,
    project_weight,
    output_weight,
    expand_weight,
    expand_bias,
    contract_weight,
    neigh_source,
    neigh_rows,
    neigh_count,
    expander_source,
    expander_rows,
    expander_count,
):
    span = lax.axis_size("nodes")
    me = lax.axis_index("nodes").astype(jnp.int32)
    shares = lax.axis_size("heads")
    share = lax.axis_index("heads").astype(jnp.int32)
    core = jnp.bitwise_and(me, 1)
    blocks, neigh_tiles, block_rows = neigh_rows.shape
    rows, features = node_states.shape
    all_blocks = blocks * span
    lanes = 128
    barrier = lax.optimization_barrier

    message, slots = ask(expander_source.T, virtual_states, span)
    heard = lax.all_to_all(message, "nodes", split_axis=0, concat_axis=0, tiled=True)
    weight_t = project_weight.T
    query, packed, outer, inner, piece = project(
        core.reshape(1), node_states, weight_t, rows // 2, TIGHT, expand_weight, contract_weight
    )
    outward = [(i, (i + (1 if i % 2 else -1)) % span) for i in range(span)]
    inward = [(i, i ^ 1) for i in range(span)]

    def turn(value, by):
        return lax.ppermute(value, "heads", [(i, (i + by) % shares) for i in range(shares)])

    half = expand_weight.shape[1] // 2
    once = turn(piece, 1)
    chosen = select_blocks(me.reshape(1), heard, packed)
    chosen, heard, outer, inner = barrier((chosen, heard, outer, inner))
    replies = lax.all_to_all(
        chosen.reshape(span, BCAP * block_rows, lanes),
        "nodes",
        split_axis=0,
        concat_axis=0,
        tiled=True,
    ).reshape(span * BCAP, block_rows, lanes)

    inner = lax.ppermute(inner, "nodes", inward)
    outer = lax.ppermute(outer, "nodes", outward)
    extra = jnp.concatenate(
        [
            heard[:, 8 : 8 + features // lanes].reshape(span, features),
            jnp.zeros((block_rows - span, features), bf16),
        ],
        axis=0,
    )
    _, virtual_packed = project(core.reshape(1), extra, weight_t, block_rows, 16)
    piece, once, virtual_packed = barrier((piece, once, virtual_packed))
    local_ids = jnp.arange(blocks, dtype=jnp.int32)[:, None]
    global_ids = me * blocks + local_ids
    place = jnp.mod(neigh_source - global_ids + 1, all_blocks) + local_ids - 1
    edge = core * (blocks - 1)
    beyond = jnp.where(core == 0, place < 0, place == blocks)
    place = jnp.where(beyond, 0, jnp.where(place < 0, blocks, place))
    near_count = jnp.where(beyond, 0, neigh_count)
    edge_count = jnp.where(beyond, neigh_count, 0)
    near_sum, near_total = near_terms(
        place.reshape(-1),
        near_count.reshape(-1),
        query,
        packed,
        inner,
        virtual_packed,
        neigh_rows,
        4,
    )

    back = turn(piece, -1)
    pieces = [piece, once, back]
    for step in range(2, 4):
        pieces += [turn(pieces[-2], 1), turn(pieces[-1], -1)]
    pieces.append(turn(piece, 4))
    offsets = (0, -1, 1, -2, 2, -3, 3, -4)
    mine = jnp.stack(pieces)
    mine, near_total, outer = barrier((mine, near_total, outer))
    theirs = lax.ppermute(mine, "nodes", inward)

    attended = far_terms(
        share.reshape(1),
        slots,
        expander_count.reshape(-1),
        edge.reshape(1),
        edge_count.reshape(-1),
        query,
        replies,
        expander_rows,
        outer,
        neigh_rows,
        near_sum,
        near_total,
        shares,
        16,
    )
    own, output_staged, mine, theirs = stage(
        share.reshape(1), node_states, rows // shares, output_weight, mine, theirs
    )
    regrouped = [attended[0]] + [None] * (shares - 1)
    for ahead in sorted(range(1, shares), key=lambda ahead: -min(ahead, shares - ahead)):
        regrouped[ahead] = lax.ppermute(
            attended[ahead], "heads", [(i, (i + ahead) % shares) for i in range(shares)]
        )
    return tail(
        jnp.stack([share, core]),
        own,
        output_staged,
        mine,
        theirs,
        expand_bias.reshape(2 * shares, 1, half),
        regrouped,
        offsets,
    )


def solution(mesh):
    return jax.shard_map(
        local,
        mesh=mesh,
        in_specs=(
            P("nodes", None),
            P("nodes", None),
            P(None, "heads"),
            P(),
            P(None, "heads"),
            P(),
            P("heads", None),
            P("nodes", None),
            P("nodes", None, None),
            P("nodes", None),
            P("nodes", None),
            P("nodes", None, None),
            P("nodes", None),
        ),
        out_specs=P(("nodes", "heads"), None),
        check_vma=False,
    )
```

```python
import functools

import jax
import jax.numpy as jnp
from jax import lax
from jax.experimental import pallas as pl
from jax.experimental.pallas import tpu as pltpu
from jax.sharding import PartitionSpec as P

HEAD_DIM = 64
BCAP = 4

eps_norm = 1e-05
clip_level = 5.0
TAIL = 10
STAGE = 16
SELECT = 53
TIGHT = 58

f32 = jnp.float32
bf16 = jnp.bfloat16
def params(mib):
    return pltpu.CompilerParams(vmem_limit_bytes=mib * 2**20)


def layer_norm(values):
    values = values.astype(f32)
    center = values - jnp.mean(values, axis=-1, keepdims=True)
    spread = jnp.mean(center * center, axis=-1, keepdims=True)
    return center * lax.rsqrt(spread + eps_norm)


vmem = pl.BlockSpec(memory_space=pltpu.VMEM)
smem = pl.BlockSpec(memory_space=pltpu.SMEM)


def ask_kernel(source_ref, virtual_ref, out_ref, slot_ref, table_ref):
    tiles, blocks = source_ref.shape
    span, _, lanes = out_ref.shape
    bits = blocks.bit_length() - 1
    source = jnp.concatenate([source_ref[t : t + 1, :] for t in range(tiles)], axis=1)
    across = jnp.broadcast_to(source, (lanes, lanes))
    down = across.T
    up = lax.broadcasted_iota(jnp.int32, (lanes, lanes), 0)
    along = lax.broadcasted_iota(jnp.int32, (lanes, lanes), 1)
    again = jnp.where((across == down) & (along < up), 1.0, 0.0)
    first = jnp.sum(again, axis=1, keepdims=True) == 0.0
    same = lax.shift_right_logical(across, bits) == lax.shift_right_logical(down, bits)
    below = jnp.where(same & (down < across) & first, 1.0, 0.0)
    rank = jnp.sum(below, axis=0, keepdims=True).astype(jnp.int32)
    slot = lax.shift_right_logical(source, bits) * BCAP + rank
    slot_ref[...] = slot
    slot_down = jnp.broadcast_to(slot, (lanes, lanes)).T
    place = jnp.where((slot_down == along) & first, (down & (blocks - 1)).astype(f32), 0.0)
    table_ref[...] = jnp.zeros_like(table_ref)
    table_ref[0:1, :] = jnp.sum(place, axis=0, keepdims=True)
    for part in range(virtual_ref.shape[1] // lanes):
        table_ref[8 + part : 9 + part, :] = virtual_ref[
            :, part * lanes : (part + 1) * lanes
        ].astype(f32)
    table = table_ref[...].astype(bf16)
    for item in range(span):
        out_ref[item] = table


def ask(source, virtual_states, span):
    lanes = 128
    return pl.pallas_call(
        ask_kernel,
        in_specs=[vmem, vmem],
        out_specs=[vmem, vmem],
        out_shape=[
            jax.ShapeDtypeStruct((span, 16, lanes), bf16),
            jax.ShapeDtypeStruct((1, lanes), jnp.int32),
        ],
        scratch_shapes=[pltpu.VMEM((16, lanes), f32)],
        compiler_params=params(56),
        name="ask",
    )(source, virtual_states)


def project_kernel(core_ref, x_ref, w_ref, *refs):
    query_ref, pack_ref = refs[2:4] if len(refs) > 2 else refs
    rest = refs
    head = HEAD_DIM
    wide = 2 * head
    rows = min(x_ref.shape[0], 512)
    for start in range(0, x_ref.shape[0], rows):
        normed = layer_norm(x_ref[start : start + rows, :]).astype(bf16)
        sides = lax.dot_general(
            w_ref[...], normed, (((1,), (1,)), ((), ())), preferred_element_type=f32
        ).astype(bf16)
        query_ref[:, start : start + rows] = sides[:head] * jnp.asarray(head**-0.5, bf16)
        for item in range(rows // wide):
            pack_ref[start // wide + item] = sides[head:, item * wide : (item + 1) * wide]
    if len(rest) > 2:
        expand_ref, contract_ref, _, _, outer_ref, inner_ref, piece_ref = rest
        first = pl.program_id(0) == 0
        last = pl.program_id(0) == pl.num_programs(0) - 1
        even = core_ref[0] == 0
        units = piece_ref.shape[0] // 2
        for core in range(2):

            @pl.when(first & (core_ref[0] == core))
            def _():
                span = slice(core * units, (core + 1) * units)
                piece_ref[:units] = expand_ref[:, span].T
                piece_ref[units:] = contract_ref[span, :]

        @pl.when(first & even)
        def _():
            outer_ref[0] = pack_ref[0]

        @pl.when(first & jnp.logical_not(even))
        def _():
            inner_ref[0] = pack_ref[0]

        @pl.when(last & even)
        def _():
            inner_ref[0] = pack_ref[pack_ref.shape[0] - 1]

        @pl.when(last & jnp.logical_not(even))
        def _():
            outer_ref[0] = pack_ref[pack_ref.shape[0] - 1]


def project(core, states, weight_t, step_rows, mib, *feed):
    rows, features = states.shape
    wide = 2 * HEAD_DIM
    whole = [pl.BlockSpec(array.shape, lambda i: (0, 0)) for array in feed]
    more_specs, more_shapes = [], []
    if feed:
        more_specs = [pl.BlockSpec((1, wide, wide), lambda i: (0, 0, 0))] * 2
        more_specs.append(pl.BlockSpec((wide * 2, features), lambda i: (0, 0)))
        more_shapes = [jax.ShapeDtypeStruct((1, wide, wide), bf16)] * 2
        more_shapes.append(jax.ShapeDtypeStruct((wide * 2, features), bf16))
    return pl.pallas_call(
        project_kernel,
        grid=(rows // step_rows,),
        in_specs=[
            smem,
            pl.BlockSpec((step_rows, features), lambda i: (i, 0)),
            pl.BlockSpec(weight_t.shape, lambda i: (0, 0)),
        ]
        + whole,
        out_specs=[
            pl.BlockSpec((HEAD_DIM, step_rows), lambda i: (0, i)),
            pl.BlockSpec((step_rows // wide, wide, wide), lambda i: (i, 0, 0)),
        ]
        + more_specs,
        out_shape=[
            jax.ShapeDtypeStruct((HEAD_DIM, rows), bf16),
            jax.ShapeDtypeStruct((rows // wide, wide, wide), bf16),
        ]
        + more_shapes,
        compiler_params=params(mib),
        cost_estimate=pl.CostEstimate(flops=1, bytes_accessed=1, transcendentals=0),
        name="project",
    )(core, states, weight_t, *feed)


def select_kernel(
    me_ref, heard_ref, pack_ref, out_ref, heard_buf, pack_buf, table_ref, place_ref, copy_sem, sems
):
    span = heard_ref.shape[0]
    fetch_pack = pltpu.make_async_copy(pack_ref, pack_buf, sems.at[0])
    fetch_heard = pltpu.make_async_copy(heard_ref, heard_buf, sems.at[1])
    fetch_heard.start()
    fetch_pack.start()
    fetch_heard.wait()
    table_ref[...] = heard_buf[:, 0, :].astype(f32).astype(jnp.int32)
    fetch_place = pltpu.make_async_copy(table_ref, place_ref, sems.at[2])
    fetch_place.start()
    fetch_place.wait()
    fetch_pack.wait()
    base = me_ref[0] * BCAP

    def send(item, _):
        for slot in range(BCAP):
            pltpu.make_async_copy(
                pack_buf.at[place_ref[item, base + slot]],
                out_ref.at[item * BCAP + slot],
                copy_sem,
            ).start()
        return 0

    lax.fori_loop(0, span, send, 0, unroll=2)
    pltpu.make_async_copy(out_ref, out_ref, copy_sem).wait()


def select_blocks(me, heard, packed):
    span, _, lanes = heard.shape
    anywhere = pl.BlockSpec(memory_space=pl.ANY)
    return pl.pallas_call(
        select_kernel,
        in_specs=[smem, anywhere, anywhere],
        out_specs=anywhere,
        out_shape=jax.ShapeDtypeStruct((span * BCAP,) + packed.shape[1:], bf16),
        scratch_shapes=[
            pltpu.VMEM(heard.shape, bf16),
            pltpu.VMEM(packed.shape, bf16),
            pltpu.VMEM((span, lanes), jnp.int32),
            pltpu.SMEM((span, lanes), jnp.int32),
            pltpu.SemaphoreType.DMA,
            pltpu.SemaphoreType.DMA((3,)),
        ],
        compiler_params=params(SELECT),
        name="select_blocks",
    )(me, heard, packed)


def tile_terms(query, blocks, rows, counts):
    head = HEAD_DIM
    wide = 2 * head
    lane = lax.broadcasted_iota(jnp.int32, (1, wide), 1)
    spot = lax.broadcasted_iota(jnp.int32, (wide, wide), 0)
    summed, total = None, None
    for block, row, count in zip(blocks, rows, counts):
        pick = jnp.where(spot == row, 1.0, 0.0).astype(bf16)
        pairs = jnp.dot(block, pick, preferred_element_type=f32)
        score = jnp.sum(pairs[:head] * query, axis=0, keepdims=True)
        weight = jnp.exp(jnp.clip(score, -clip_level, clip_level))
        weight = jnp.where(lane < count, weight, 0.0)
        value = pairs[head:] * weight
        summed = value if summed is None else summed + value
        total = weight if total is None else total + weight
    return summed, total


def tile_rows(rows_ref, block):
    rows = rows_ref[block]
    return [rows[tile : tile + 1] for tile in range(rows.shape[0])]


def near_kernel(
    group, place_ref, count_ref, query_ref, pack_ref, inner_ref, virtual_ref, rows_ref, sum_ref,
    total_ref, window_ref,
):
    head = HEAD_DIM
    blocks, tiles, wide = rows_ref.shape
    virtual_total = 32
    virtual_keys = virtual_ref[0, :head, :].T[:virtual_total]
    virtual_values = virtual_ref[0, head:, :virtual_total]
    window_ref[blocks] = inner_ref[0]

    def fill(block, _):
        window_ref[block] = pack_ref[block]
        return 0

    lax.fori_loop(0, blocks, fill, 0, unroll=8)

    def step(turn, _):
        for item in range(group):
            block = turn * group + item
            lanes = pl.ds(pl.multiple_of(block * wide, wide), wide)
            query = query_ref[:, lanes]
            tile_blocks = [window_ref[place_ref[block, t]] for t in range(tiles)]
            counts = [count_ref[block, t] for t in range(tiles)]
            summed, total = tile_terms(
                query.astype(f32), tile_blocks, tile_rows(rows_ref, block), counts
            )
            scores = jnp.dot(virtual_keys, query, preferred_element_type=f32)
            weights = jnp.exp(jnp.clip(scores, -clip_level, clip_level))
            total = total + jnp.sum(weights, axis=0, keepdims=True)
            summed = summed + jnp.dot(
                virtual_values, weights.astype(bf16), preferred_element_type=f32
            )
            sum_ref[:, lanes] = summed
            total_ref[:, lanes] = total
        return 0

    lax.fori_loop(0, blocks // group, step, 0)


def near_terms(places, counts, query, packed, inner, virtual, rows, group):
    head, total = query.shape
    blocks = packed.shape[0]
    return pl.pallas_call(
        functools.partial(near_kernel, group),
        in_specs=[smem, smem] + [vmem] * 5,
        out_specs=[vmem, vmem],
        out_shape=[
            jax.ShapeDtypeStruct((head, total), f32),
            jax.ShapeDtypeStruct((1, total), f32),
        ],
        scratch_shapes=[pltpu.VMEM((blocks + 1,) + packed.shape[1:], bf16)],
        compiler_params=params(TIGHT),
        cost_estimate=pl.CostEstimate(flops=1, bytes_accessed=1, transcendentals=0),
        name="near_terms",
    )(places, counts, query, packed, inner, virtual, rows)


def far_kernel(
    group, share_ref, slot_ref, count_ref, edge_ref, edge_count_ref, query_ref, reply_ref, rows_ref,
    outer_ref, edge_rows_ref, sum_ref, total_ref, *rest
):
    outs, (out_ref, sem) = rest[:-2], rest[-2:]
    blocks, tiles, wide = rows_ref.shape
    share_blocks = blocks // out_ref.shape[0]
    edge = edge_ref[0]
    near_tiles = edge_rows_ref.shape[1]
    edge_sum, edge_total = tile_terms(
        query_ref[:, pl.ds(pl.multiple_of(edge * wide, wide), wide)].astype(f32),
        [outer_ref[0]] * near_tiles,
        tile_rows(edge_rows_ref, edge),
        [edge_count_ref[edge, t] for t in range(near_tiles)],
    )

    def step(turn, _):
        for item in range(group):
            block = turn * group + item
            lanes = pl.ds(pl.multiple_of(block * wide, wide), wide)
            tile_blocks = [reply_ref[slot_ref[0, t * blocks + block]] for t in range(tiles)]
            counts = [count_ref[block, t] for t in range(tiles)]
            summed, total = tile_terms(
                query_ref[:, lanes].astype(f32), tile_blocks, tile_rows(rows_ref, block), counts
            )
            here = (block == edge).astype(f32)
            total = total + total_ref[:, lanes] + here * edge_total
            result = (summed + sum_ref[:, lanes] + here * edge_sum) * (1.0 / total)
            inner = pl.ds(pl.multiple_of(lax.rem(block, share_blocks) * wide, wide), wide)
            out_ref[lax.div(block, share_blocks), :, inner] = result.astype(bf16)
        return 0

    lax.fori_loop(0, blocks // group, step, 0)
    copies = []
    for ahead, out in enumerate(outs):
        share = lax.rem(share_ref[0] + ahead, len(outs))
        copies.append(pltpu.make_async_copy(out_ref.at[share], out, sem.at[ahead]))
        copies[-1].start()
    for copy in copies:
        copy.wait()


def far_terms(
    share, slots, counts, edge, edge_counts, query, replies, rows, outer, edge_rows, near_sum,
    near_total, shares, group,
):
    head, total = query.shape
    return pl.pallas_call(
        functools.partial(far_kernel, group),
        in_specs=[smem] * 5 + [vmem] * 7,
        out_specs=[pl.BlockSpec(memory_space=pl.ANY)] * shares,
        out_shape=[jax.ShapeDtypeStruct((head, total // shares), bf16)] * shares,
        scratch_shapes=[
            pltpu.VMEM((shares, head, total // shares), bf16),
            pltpu.SemaphoreType.DMA((shares,)),
        ],
        compiler_params=params(TIGHT),
        name="far_terms",
    )(
        share, slots, counts, edge, edge_counts, query, replies, rows, outer, edge_rows, near_sum,
        near_total,
    )


def stage_kernel(share_ref, states_ref, *refs):
    sources, (own_ref, *copies, sems) = refs[:3], refs[3:]
    rows = own_ref.shape[0]
    start = pl.multiple_of(share_ref[0] * rows, rows)
    fetches = [pltpu.make_async_copy(states_ref.at[pl.ds(start, rows)], own_ref, sems.at[0])]
    for item, (source, copy) in enumerate(zip(sources, copies)):
        fetches.append(pltpu.make_async_copy(source, copy, sems.at[item + 1]))
    for fetch in fetches:
        fetch.start()
    for fetch in fetches:
        fetch.wait()


def stage(share, states, rows, *others):
    return pl.pallas_call(
        stage_kernel,
        in_specs=[smem] + [pl.BlockSpec(memory_space=pl.ANY)] * (1 + len(others)),
        out_specs=[vmem] * (1 + len(others)),
        out_shape=[jax.ShapeDtypeStruct((rows, states.shape[1]), bf16)]
        + [jax.ShapeDtypeStruct(other.shape, bf16) for other in others],
        scratch_shapes=[pltpu.SemaphoreType.DMA((1 + len(others),))],
        compiler_params=params(STAGE),
        name="stage",
    )(share, states, *others)


def tail_kernel(
    offsets, place_ref, own_ref, output_ref, mine_ref, theirs_ref, bias_ref, *rest
):
    pieces, (out_ref, att_ref) = rest[:-2], rest[-2:]
    features, rows = att_ref.shape
    head, _ = pieces[0].shape
    for behind, piece in enumerate(pieces):
        owner = lax.rem(place_ref[0] + len(pieces) - behind, len(pieces))
        att_ref[pl.ds(pl.multiple_of(owner * head, head), head), :] = piece[...]
    parts = len(offsets)
    wide = mine_ref.shape[1] // 2
    attended = att_ref[...].T
    residual = own_ref[...].astype(f32) + jnp.dot(
        attended, output_ref[...], preferred_element_type=f32
    )
    normed = layer_norm(residual).astype(bf16)
    summed = residual
    for part, offset in enumerate(offsets):
        owner = lax.rem(place_ref[0] + offset + parts, parts)
        bias = jnp.concatenate(
            [bias_ref[2 * owner + place_ref[1]], bias_ref[2 * owner + 1 - place_ref[1]]], axis=1
        )
        first = jnp.concatenate([mine_ref[part, :wide], theirs_ref[part, :wide]], axis=0)
        second = jnp.concatenate([mine_ref[part, wide:], theirs_ref[part, wide:]], axis=0)
        inner = lax.dot_general(
            normed, first, (((1,), (1,)), ((), ())), preferred_element_type=f32
        )
        inner = inner + bias
        hidden = ((inner * 0.5) * (1.0 + lax.erf(inner * (0.5**0.5)))).astype(bf16)
        summed = summed + jnp.dot(hidden, second, preferred_element_type=f32)
    out_ref[...] = summed.astype(bf16)


def tail(place, own, output_weight, mine, theirs, bias, pieces, offsets):
    rows, features = own.shape
    return pl.pallas_call(
        functools.partial(tail_kernel, offsets),
        in_specs=[smem] + [vmem] * (5 + len(pieces)),
        out_specs=vmem,
        out_shape=jax.ShapeDtypeStruct(own.shape, bf16),
        scratch_shapes=[pltpu.VMEM((features, rows), bf16)],
        compiler_params=params(TAIL),
        name="tail",
    )(place, own, output_weight, mine, theirs, bias, *pieces)


def local(
    node_states,
    virtual_states,
    project_weight,
    output_weight,
    expand_weight,
    expand_bias,
    contract_weight,
    neigh_source,
    neigh_rows,
    neigh_count,
    expander_source,
    expander_rows,
    expander_count,
):
    span = lax.axis_size("nodes")
    me = lax.axis_index("nodes").astype(jnp.int32)
    shares = lax.axis_size("heads")
    share = lax.axis_index("heads").astype(jnp.int32)
    core = jnp.bitwise_and(me, 1)
    blocks, neigh_tiles, block_rows = neigh_rows.shape
    rows, features = node_states.shape
    all_blocks = blocks * span
    lanes = 128
    barrier = lax.optimization_barrier

    message, slots = ask(expander_source.T, virtual_states, span)
    heard = lax.all_to_all(message, "nodes", split_axis=0, concat_axis=0, tiled=True)
    weight_t = project_weight.T
    query, packed, outer, inner, piece = project(
        core.reshape(1), node_states, weight_t, rows // 2, TIGHT, expand_weight, contract_weight
    )
    outward = [(i, (i + (1 if i % 2 else -1)) % span) for i in range(span)]
    inward = [(i, i ^ 1) for i in range(span)]

    def turn(value, by):
        return lax.ppermute(value, "heads", [(i, (i + by) % shares) for i in range(shares)])

    half = expand_weight.shape[1] // 2
    chosen = select_blocks(me.reshape(1), heard, packed)
    chosen, heard, outer, inner = barrier((chosen, heard, outer, inner))
    replies = lax.all_to_all(
        chosen.reshape(span, BCAP * block_rows, lanes),
        "nodes",
        split_axis=0,
        concat_axis=0,
        tiled=True,
    ).reshape(span * BCAP, block_rows, lanes)

    inner = lax.ppermute(inner, "nodes", inward)
    outer = lax.ppermute(outer, "nodes", outward)
    extra = jnp.concatenate(
        [
            heard[:, 8 : 8 + features // lanes].reshape(span, features),
            jnp.zeros((block_rows - span, features), bf16),
        ],
        axis=0,
    )
    _, virtual_packed = project(core.reshape(1), extra, weight_t, block_rows, 16)
    piece, virtual_packed = barrier((piece, virtual_packed))
    local_ids = jnp.arange(blocks, dtype=jnp.int32)[:, None]
    global_ids = me * blocks + local_ids
    place = jnp.mod(neigh_source - global_ids + 1, all_blocks) + local_ids - 1
    edge = core * (blocks - 1)
    beyond = jnp.where(core == 0, place < 0, place == blocks)
    place = jnp.where(beyond, 0, jnp.where(place < 0, blocks, place))
    near_count = jnp.where(beyond, 0, neigh_count)
    edge_count = jnp.where(beyond, neigh_count, 0)
    near_sum, near_total = near_terms(
        place,
        near_count,
        query,
        packed,
        inner,
        virtual_packed,
        neigh_rows,
        4,
    )

    once, back = turn(piece, 1), turn(piece, -1)
    pieces = [piece, once, back]
    for step in range(2, 4):
        pieces += [turn(pieces[-2], 1), turn(pieces[-1], -1)]
    pieces.append(turn(piece, 4))
    offsets = (0, -1, 1, -2, 2, -3, 3, -4)
    mine = jnp.stack(pieces)
    theirs = lax.ppermute(mine, "nodes", inward)

    attended = far_terms(
        share.reshape(1),
        slots,
        expander_count,
        edge.reshape(1),
        edge_count,
        query,
        replies,
        expander_rows,
        outer,
        neigh_rows,
        near_sum,
        near_total,
        shares,
        16,
    )
    own, output_staged, mine, theirs = stage(
        share.reshape(1), node_states, rows // shares, output_weight, mine, theirs
    )
    regrouped = [attended[0]] + [None] * (shares - 1)
    for ahead in sorted(range(1, shares), key=lambda ahead: -min(ahead, shares - ahead)):
        regrouped[ahead] = lax.ppermute(
            attended[ahead], "heads", [(i, (i + ahead) % shares) for i in range(shares)]
        )
    return tail(
        jnp.stack([share, core]),
        own,
        output_staged,
        mine,
        theirs,
        expand_bias.reshape(2 * shares, 1, half),
        regrouped,
        offsets,
    )


def solution(mesh):
    return jax.shard_map(
        local,
        mesh=mesh,
        in_specs=(
            P("nodes", None),
            P("nodes", None),
            P(None, "heads"),
            P(),
            P(None, "heads"),
            P(),
            P("heads", None),
            P("nodes", None),
            P("nodes", None, None),
            P("nodes", None),
            P("nodes", None),
            P("nodes", None, None),
            P("nodes", None),
        ),
        out_specs=P(("nodes", "heads"), None),
        check_vma=False,
    )
```

```python
import functools

import jax
import jax.numpy as jnp
from jax import lax
from jax.experimental import pallas as pl
from jax.experimental.pallas import tpu as pltpu
from jax.sharding import PartitionSpec as P

HEAD_DIM = 64
BCAP = 4

eps_norm = 1e-05
clip_level = 5.0
TAIL = 10
STAGE = 16
SELECT = 53
TIGHT = 58

f32 = jnp.float32
bf16 = jnp.bfloat16
def params(mib):
    return pltpu.CompilerParams(vmem_limit_bytes=mib * 2**20)


def layer_norm(values):
    values = values.astype(f32)
    center = values - jnp.mean(values, axis=-1, keepdims=True)
    spread = jnp.mean(center * center, axis=-1, keepdims=True)
    return center * lax.rsqrt(spread + eps_norm)


vmem = pl.BlockSpec(memory_space=pltpu.VMEM)
smem = pl.BlockSpec(memory_space=pltpu.SMEM)


def ask_kernel(source_ref, virtual_ref, out_ref, slot_ref, table_ref):
    tiles, blocks = source_ref.shape
    span, _, lanes = out_ref.shape
    bits = blocks.bit_length() - 1
    source = jnp.concatenate([source_ref[t : t + 1, :] for t in range(tiles)], axis=1)
    across = jnp.broadcast_to(source, (lanes, lanes))
    down = across.T
    up = lax.broadcasted_iota(jnp.int32, (lanes, lanes), 0)
    along = lax.broadcasted_iota(jnp.int32, (lanes, lanes), 1)
    again = jnp.where((across == down) & (along < up), 1.0, 0.0)
    first = jnp.sum(again, axis=1, keepdims=True) == 0.0
    same = lax.shift_right_logical(across, bits) == lax.shift_right_logical(down, bits)
    below = jnp.where(same & (down < across) & first, 1.0, 0.0)
    rank = jnp.sum(below, axis=0, keepdims=True).astype(jnp.int32)
    slot = lax.shift_right_logical(source, bits) * BCAP + rank
    slot_ref[...] = slot
    slot_down = jnp.broadcast_to(slot, (lanes, lanes)).T
    place = jnp.where((slot_down == along) & first, (down & (blocks - 1)).astype(f32), 0.0)
    table_ref[...] = jnp.zeros_like(table_ref)
    table_ref[0:1, :] = jnp.sum(place, axis=0, keepdims=True)
    for part in range(virtual_ref.shape[1] // lanes):
        table_ref[8 + part : 9 + part, :] = virtual_ref[
            :, part * lanes : (part + 1) * lanes
        ].astype(f32)
    table = table_ref[...].astype(bf16)
    for item in range(span):
        out_ref[item] = table


def ask(source, virtual_states, span):
    lanes = 128
    return pl.pallas_call(
        ask_kernel,
        in_specs=[vmem, vmem],
        out_specs=[vmem, vmem],
        out_shape=[
            jax.ShapeDtypeStruct((span, 16, lanes), bf16),
            jax.ShapeDtypeStruct((1, lanes), jnp.int32),
        ],
        scratch_shapes=[pltpu.VMEM((16, lanes), f32)],
        compiler_params=params(56),
        name="ask",
    )(source, virtual_states)


def project_kernel(core_ref, x_ref, w_ref, *refs):
    query_ref, pack_ref = refs[2:4] if len(refs) > 2 else refs
    rest = refs
    head = HEAD_DIM
    wide = 2 * head
    rows = min(x_ref.shape[0], 512)
    for start in range(0, x_ref.shape[0], rows):
        normed = layer_norm(x_ref[start : start + rows, :]).astype(bf16)
        sides = lax.dot_general(
            w_ref[...], normed, (((1,), (1,)), ((), ())), preferred_element_type=f32
        ).astype(bf16)
        query_ref[:, start : start + rows] = sides[:head] * jnp.asarray(head**-0.5, bf16)
        for item in range(rows // wide):
            pack_ref[start // wide + item] = sides[head:, item * wide : (item + 1) * wide]
    if len(rest) > 2:
        expand_ref, contract_ref, _, _, outer_ref, inner_ref, piece_ref = rest
        first = pl.program_id(0) == 0
        last = pl.program_id(0) == pl.num_programs(0) - 1
        even = core_ref[0] == 0
        units = piece_ref.shape[0] // 2
        for core in range(2):

            @pl.when(first & (core_ref[0] == core))
            def _():
                span = slice(core * units, (core + 1) * units)
                piece_ref[:units] = expand_ref[:, span].T
                piece_ref[units:] = contract_ref[span, :]

        @pl.when(first & even)
        def _():
            outer_ref[0] = pack_ref[0]

        @pl.when(first & jnp.logical_not(even))
        def _():
            inner_ref[0] = pack_ref[0]

        @pl.when(last & even)
        def _():
            inner_ref[0] = pack_ref[pack_ref.shape[0] - 1]

        @pl.when(last & jnp.logical_not(even))
        def _():
            outer_ref[0] = pack_ref[pack_ref.shape[0] - 1]


def project(core, states, weight_t, step_rows, mib, *feed):
    rows, features = states.shape
    wide = 2 * HEAD_DIM
    whole = [pl.BlockSpec(array.shape, lambda i: (0, 0)) for array in feed]
    more_specs, more_shapes = [], []
    if feed:
        more_specs = [pl.BlockSpec((1, wide, wide), lambda i: (0, 0, 0))] * 2
        more_specs.append(pl.BlockSpec((wide * 2, features), lambda i: (0, 0)))
        more_shapes = [jax.ShapeDtypeStruct((1, wide, wide), bf16)] * 2
        more_shapes.append(jax.ShapeDtypeStruct((wide * 2, features), bf16))
    return pl.pallas_call(
        project_kernel,
        grid=(rows // step_rows,),
        in_specs=[
            smem,
            pl.BlockSpec((step_rows, features), lambda i: (i, 0)),
            pl.BlockSpec(weight_t.shape, lambda i: (0, 0)),
        ]
        + whole,
        out_specs=[
            pl.BlockSpec((HEAD_DIM, step_rows), lambda i: (0, i)),
            pl.BlockSpec((step_rows // wide, wide, wide), lambda i: (i, 0, 0)),
        ]
        + more_specs,
        out_shape=[
            jax.ShapeDtypeStruct((HEAD_DIM, rows), bf16),
            jax.ShapeDtypeStruct((rows // wide, wide, wide), bf16),
        ]
        + more_shapes,
        compiler_params=params(mib),
        cost_estimate=pl.CostEstimate(flops=1, bytes_accessed=1, transcendentals=0),
        name="project",
    )(core, states, weight_t, *feed)


def select_kernel(
    me_ref, heard_ref, pack_ref, out_ref, heard_buf, pack_buf, table_ref, place_ref, copy_sem, sems
):
    span = heard_ref.shape[0]
    fetch_pack = pltpu.make_async_copy(pack_ref, pack_buf, sems.at[0])
    fetch_heard = pltpu.make_async_copy(heard_ref, heard_buf, sems.at[1])
    fetch_heard.start()
    fetch_pack.start()
    fetch_heard.wait()
    table_ref[...] = heard_buf[:, 0, :].astype(f32).astype(jnp.int32)
    fetch_place = pltpu.make_async_copy(table_ref, place_ref, sems.at[2])
    fetch_place.start()
    fetch_place.wait()
    fetch_pack.wait()
    base = me_ref[0] * BCAP

    def send(item, _):
        for slot in range(BCAP):
            pltpu.make_async_copy(
                pack_buf.at[place_ref[item, base + slot]],
                out_ref.at[item * BCAP + slot],
                copy_sem,
            ).start()
        return 0

    lax.fori_loop(0, span, send, 0, unroll=2)
    pltpu.make_async_copy(out_ref, out_ref, copy_sem).wait()


def select_blocks(me, heard, packed):
    span, _, lanes = heard.shape
    anywhere = pl.BlockSpec(memory_space=pl.ANY)
    return pl.pallas_call(
        select_kernel,
        in_specs=[smem, anywhere, anywhere],
        out_specs=anywhere,
        out_shape=jax.ShapeDtypeStruct((span * BCAP,) + packed.shape[1:], bf16),
        scratch_shapes=[
            pltpu.VMEM(heard.shape, bf16),
            pltpu.VMEM(packed.shape, bf16),
            pltpu.VMEM((span, lanes), jnp.int32),
            pltpu.SMEM((span, lanes), jnp.int32),
            pltpu.SemaphoreType.DMA,
            pltpu.SemaphoreType.DMA((3,)),
        ],
        compiler_params=params(SELECT),
        name="select_blocks",
    )(me, heard, packed)


def tile_terms(query, blocks, rows, counts):
    head = HEAD_DIM
    wide = 2 * head
    lane = lax.broadcasted_iota(jnp.int32, (1, wide), 1)
    spot = lax.broadcasted_iota(jnp.int32, (wide, wide), 0)
    summed, total = None, None
    for block, row, count in zip(blocks, rows, counts):
        pick = jnp.where(spot == row, 1.0, 0.0).astype(bf16)
        pairs = jnp.dot(block, pick, preferred_element_type=f32)
        score = jnp.sum(pairs[:head] * query, axis=0, keepdims=True)
        weight = jnp.exp(jnp.clip(score, -clip_level, clip_level))
        weight = jnp.where(lane < count, weight, 0.0)
        value = pairs[head:] * weight
        summed = value if summed is None else summed + value
        total = weight if total is None else total + weight
    return summed, total


def tile_rows(rows_ref, block):
    rows = rows_ref[block]
    return [rows[tile : tile + 1] for tile in range(rows.shape[0])]


def near_kernel(
    group, place_ref, count_ref, query_ref, pack_ref, inner_ref, virtual_ref, rows_ref, sum_ref,
    total_ref, window_ref,
):
    head = HEAD_DIM
    blocks, tiles, wide = rows_ref.shape
    virtual_total = 32
    virtual_keys = virtual_ref[0, :head, :].T[:virtual_total]
    virtual_values = virtual_ref[0, head:, :virtual_total]
    window_ref[blocks] = inner_ref[0]

    def fill(block, _):
        window_ref[block] = pack_ref[block]
        return 0

    lax.fori_loop(0, blocks, fill, 0, unroll=8)

    def step(turn, _):
        for item in range(group):
            block = turn * group + item
            lanes = pl.ds(pl.multiple_of(block * wide, wide), wide)
            query = query_ref[:, lanes]
            tile_blocks = [window_ref[place_ref[block, t]] for t in range(tiles)]
            counts = [count_ref[block, t] for t in range(tiles)]
            summed, total = tile_terms(
                query.astype(f32), tile_blocks, tile_rows(rows_ref, block), counts
            )
            scores = jnp.dot(virtual_keys, query, preferred_element_type=f32)
            weights = jnp.exp(jnp.clip(scores, -clip_level, clip_level))
            total = total + jnp.sum(weights, axis=0, keepdims=True)
            summed = summed + jnp.dot(
                virtual_values, weights.astype(bf16), preferred_element_type=f32
            )
            sum_ref[:, lanes] = summed
            total_ref[:, lanes] = total
        return 0

    lax.fori_loop(0, blocks // group, step, 0)


def near_terms(places, counts, query, packed, inner, virtual, rows, group):
    head, total = query.shape
    blocks = packed.shape[0]
    return pl.pallas_call(
        functools.partial(near_kernel, group),
        in_specs=[smem, smem] + [vmem] * 5,
        out_specs=[vmem, vmem],
        out_shape=[
            jax.ShapeDtypeStruct((head, total), f32),
            jax.ShapeDtypeStruct((1, total), f32),
        ],
        scratch_shapes=[pltpu.VMEM((blocks + 1,) + packed.shape[1:], bf16)],
        compiler_params=params(TIGHT),
        cost_estimate=pl.CostEstimate(flops=1, bytes_accessed=1, transcendentals=0),
        name="near_terms",
    )(places, counts, query, packed, inner, virtual, rows)


def far_kernel(
    group, share_ref, slot_ref, count_ref, edge_ref, edge_count_ref, query_ref, reply_ref, rows_ref,
    outer_ref, edge_rows_ref, sum_ref, total_ref, *rest
):
    outs, (out_ref, sem) = rest[:-2], rest[-2:]
    blocks, tiles, wide = rows_ref.shape
    share_blocks = blocks // out_ref.shape[0]
    edge = edge_ref[0]
    near_tiles = edge_rows_ref.shape[1]
    edge_sum, edge_total = tile_terms(
        query_ref[:, pl.ds(pl.multiple_of(edge * wide, wide), wide)].astype(f32),
        [outer_ref[0]] * near_tiles,
        tile_rows(edge_rows_ref, edge),
        [edge_count_ref[edge, t] for t in range(near_tiles)],
    )

    def step(turn, _):
        for item in range(group):
            block = turn * group + item
            lanes = pl.ds(pl.multiple_of(block * wide, wide), wide)
            tile_blocks = [reply_ref[slot_ref[0, t * blocks + block]] for t in range(tiles)]
            counts = [count_ref[block, t] for t in range(tiles)]
            summed, total = tile_terms(
                query_ref[:, lanes].astype(f32), tile_blocks, tile_rows(rows_ref, block), counts
            )
            here = (block == edge).astype(f32)
            total = total + total_ref[:, lanes] + here * edge_total
            result = (summed + sum_ref[:, lanes] + here * edge_sum) * (1.0 / total)
            inner = pl.ds(pl.multiple_of(lax.rem(block, share_blocks) * wide, wide), wide)
            out_ref[lax.div(block, share_blocks), :, inner] = result.astype(bf16)
        return 0

    lax.fori_loop(0, blocks // group, step, 0)
    copies = []
    for ahead, out in enumerate(outs):
        share = lax.rem(share_ref[0] + ahead, len(outs))
        copies.append(pltpu.make_async_copy(out_ref.at[share], out, sem.at[ahead]))
        copies[-1].start()
    for copy in copies:
        copy.wait()


def far_terms(
    share, slots, counts, edge, edge_counts, query, replies, rows, outer, edge_rows, near_sum,
    near_total, shares, group,
):
    head, total = query.shape
    return pl.pallas_call(
        functools.partial(far_kernel, group),
        in_specs=[smem] * 5 + [vmem] * 7,
        out_specs=[pl.BlockSpec(memory_space=pl.ANY)] * shares,
        out_shape=[jax.ShapeDtypeStruct((head, total // shares), bf16)] * shares,
        scratch_shapes=[
            pltpu.VMEM((shares, head, total // shares), bf16),
            pltpu.SemaphoreType.DMA((shares,)),
        ],
        compiler_params=params(TIGHT),
        name="far_terms",
    )(
        share, slots, counts, edge, edge_counts, query, replies, rows, outer, edge_rows, near_sum,
        near_total,
    )


def stage_kernel(share_ref, states_ref, *refs):
    sources, (own_ref, *copies, sems) = refs[:3], refs[3:]
    rows = own_ref.shape[0]
    start = pl.multiple_of(share_ref[0] * rows, rows)
    fetches = [pltpu.make_async_copy(states_ref.at[pl.ds(start, rows)], own_ref, sems.at[0])]
    for item, (source, copy) in enumerate(zip(sources, copies)):
        fetches.append(pltpu.make_async_copy(source, copy, sems.at[item + 1]))
    for fetch in fetches:
        fetch.start()
    for fetch in fetches:
        fetch.wait()


def stage(share, states, rows, *others):
    return pl.pallas_call(
        stage_kernel,
        in_specs=[smem] + [pl.BlockSpec(memory_space=pl.ANY)] * (1 + len(others)),
        out_specs=[vmem] * (1 + len(others)),
        out_shape=[jax.ShapeDtypeStruct((rows, states.shape[1]), bf16)]
        + [jax.ShapeDtypeStruct(other.shape, bf16) for other in others],
        scratch_shapes=[pltpu.SemaphoreType.DMA((1 + len(others),))],
        compiler_params=params(STAGE),
        name="stage",
    )(share, states, *others)


def tail_kernel(
    behinds, offsets, place_ref, own_ref, output_ref, mine_ref, theirs_ref, bias_ref, *rest
):
    pieces, (out_ref, att_ref) = rest[:-2], rest[-2:]
    features, rows = att_ref.shape
    head, _ = pieces[0].shape
    for behind, piece in zip(behinds, pieces):
        owner = lax.rem(place_ref[0] + len(pieces) - behind, len(pieces))
        att_ref[pl.ds(pl.multiple_of(owner * head, head), head), :] = piece[...]
    parts = len(offsets)
    wide = mine_ref.shape[1] // 2
    attended = att_ref[...].T
    residual = own_ref[...].astype(f32) + jnp.dot(
        attended, output_ref[...], preferred_element_type=f32
    )
    normed = layer_norm(residual).astype(bf16)
    summed = residual
    for part, offset in enumerate(offsets):
        owner = lax.rem(place_ref[0] + offset + parts, parts)
        bias = jnp.concatenate(
            [bias_ref[2 * owner + place_ref[1]], bias_ref[2 * owner + 1 - place_ref[1]]], axis=1
        )
        first = jnp.concatenate([mine_ref[part, :wide], theirs_ref[part, :wide]], axis=0)
        second = jnp.concatenate([mine_ref[part, wide:], theirs_ref[part, wide:]], axis=0)
        inner = lax.dot_general(
            normed, first, (((1,), (1,)), ((), ())), preferred_element_type=f32
        )
        inner = inner + bias
        hidden = ((inner * 0.5) * (1.0 + lax.erf(inner * (0.5**0.5)))).astype(bf16)
        summed = summed + jnp.dot(hidden, second, preferred_element_type=f32)
    out_ref[...] = summed.astype(bf16)


def tail(place, own, output_weight, mine, theirs, bias, pieces, behinds, offsets):
    rows, features = own.shape
    return pl.pallas_call(
        functools.partial(tail_kernel, behinds, offsets),
        in_specs=[smem] + [vmem] * (5 + len(pieces)),
        out_specs=vmem,
        out_shape=jax.ShapeDtypeStruct(own.shape, bf16),
        scratch_shapes=[pltpu.VMEM((features, rows), bf16)],
        compiler_params=params(TAIL),
        name="tail",
    )(place, own, output_weight, mine, theirs, bias, *pieces)


def local(
    node_states,
    virtual_states,
    project_weight,
    output_weight,
    expand_weight,
    expand_bias,
    contract_weight,
    neigh_source,
    neigh_rows,
    neigh_count,
    expander_source,
    expander_rows,
    expander_count,
):
    span = lax.axis_size("nodes")
    me = lax.axis_index("nodes").astype(jnp.int32)
    shares = lax.axis_size("heads")
    share = lax.axis_index("heads").astype(jnp.int32)
    core = jnp.bitwise_and(me, 1)
    blocks, neigh_tiles, block_rows = neigh_rows.shape
    rows, features = node_states.shape
    all_blocks = blocks * span
    lanes = 128
    barrier = lax.optimization_barrier

    message, slots = ask(expander_source.T, virtual_states, span)
    heard = lax.all_to_all(message, "nodes", split_axis=0, concat_axis=0, tiled=True)
    weight_t = project_weight.T
    query, packed, outer, inner, piece = project(
        core.reshape(1), node_states, weight_t, rows // 2, TIGHT, expand_weight, contract_weight
    )
    outward = [(i, (i + (1 if i % 2 else -1)) % span) for i in range(span)]
    inward = [(i, i ^ 1) for i in range(span)]

    def turn(value, by):
        return lax.ppermute(value, "heads", [(i, (i + by) % shares) for i in range(shares)])

    half = expand_weight.shape[1] // 2
    chosen = select_blocks(me.reshape(1), heard, packed)
    chosen, heard, outer, inner = barrier((chosen, heard, outer, inner))
    replies = lax.all_to_all(
        chosen.reshape(span, BCAP * block_rows, lanes),
        "nodes",
        split_axis=0,
        concat_axis=0,
        tiled=True,
    ).reshape(span * BCAP, block_rows, lanes)

    inner = lax.ppermute(inner, "nodes", inward)
    outer = lax.ppermute(outer, "nodes", outward)
    extra = jnp.concatenate(
        [
            heard[:, 8 : 8 + features // lanes].reshape(span, features),
            jnp.zeros((block_rows - span, features), bf16),
        ],
        axis=0,
    )
    _, virtual_packed = project(core.reshape(1), extra, weight_t, block_rows, 16)
    piece, virtual_packed = barrier((piece, virtual_packed))
    local_ids = jnp.arange(blocks, dtype=jnp.int32)[:, None]
    global_ids = me * blocks + local_ids
    place = jnp.mod(neigh_source - global_ids + 1, all_blocks) + local_ids - 1
    edge = core * (blocks - 1)
    beyond = jnp.where(core == 0, place < 0, place == blocks)
    place = jnp.where(beyond, 0, jnp.where(place < 0, blocks, place))
    near_count = jnp.where(beyond, 0, neigh_count)
    edge_count = jnp.where(beyond, neigh_count, 0)
    near_sum, near_total = near_terms(
        place,
        near_count,
        query,
        packed,
        inner,
        virtual_packed,
        neigh_rows,
        4,
    )

    once, back = turn(piece, 1), turn(piece, -1)
    pieces = [piece, once, back]
    for step in range(2, 4):
        pieces += [turn(pieces[-2], 1), turn(pieces[-1], -1)]
    pieces.append(turn(piece, 4))
    offsets = (0, -1, 1, -2, 2, -3, 3, -4)
    mine = jnp.stack(pieces)
    theirs = lax.ppermute(mine, "nodes", inward)

    attended = far_terms(
        share.reshape(1),
        slots,
        expander_count,
        edge.reshape(1),
        edge_count,
        query,
        replies,
        expander_rows,
        outer,
        neigh_rows,
        near_sum,
        near_total,
        shares,
        16,
    )
    own, output_staged, mine, theirs = stage(
        share.reshape(1), node_states, rows // shares, output_weight, mine, theirs
    )
    aheads = [0] + sorted(range(1, shares), key=lambda ahead: -min(ahead, shares - ahead))
    regrouped = [attended[0]] + [turn(attended[ahead], ahead) for ahead in aheads[1:]]
    return tail(
        jnp.stack([share, core]),
        own,
        output_staged,
        mine,
        theirs,
        expand_bias.reshape(2 * shares, 1, half),
        regrouped,
        tuple(aheads),
        offsets,
    )


def solution(mesh):
    return jax.shard_map(
        local,
        mesh=mesh,
        in_specs=(
            P("nodes", None),
            P("nodes", None),
            P(None, "heads"),
            P(),
            P(None, "heads"),
            P(),
            P("heads", None),
            P("nodes", None),
            P("nodes", None, None),
            P("nodes", None),
            P("nodes", None),
            P("nodes", None, None),
            P("nodes", None),
        ),
        out_specs=P(("nodes", "heads"), None),
        check_vma=False,
    )
```
